512 devices in a mesh: sec: 8 (over z_hi, x), tile: 64 (over z_lo, y, core).
Axes of the slice: x: 4, y: 4, z: 16 (z_hi: 2, z_lo: 8; z = z_hi * 8 + z_lo), core: 2. Of those that a mesh axis runs over, the one named last changes fastest.
Arguments:
- depth: float32 [512, 8192], P('sec', 'tile'), may hold values from 0 to 2
- elevation: float32 [512, 8192], P('sec', 'tile'), may hold values from -6 to 6
- land_mask: int32 [512, 8192], P('sec', 'tile'), may hold values 0 or 1
- pressure: float32 [5, 512, 8, 1024], P(None, ('sec', 'tile')), may hold values from -6 to 6
- saturated_conductance: float32 [5, 512, 8, 1024], P(None, ('sec', 'tile')), may hold values from 0.2 to 5
Outputs:
- depth_final: float32 [512, 8192], P('sec', 'tile')
- pressure_final: float32 [5, 512, 8, 1024], P(None, ('sec', 'tile'))
The draws below stay inside these ranges and needn't reach their ends.
All inputs are finite; a program needn't handle non-finite values. No bound on the sum of `land_mask` on one device may be relied on, other than what follows from the above.
Results may differ from the reference program's by a relative error of at most 0.000035.
Values sent between devices are 32-bit elements; how exact they have to be, the bound alone decides.
No kernel may reach another device: no remote copies, remote signals or barrier semaphores. Data moves between devices by JAX's collectives and lax.ppermute only.
A program may use at most 64 MiB of HBM per device.

```python
import math
import jax
import jax.numpy as jnp

SOIL_LAYER_COUNT = 5
SWEEPS = 3
STEPS = 4
BLOCK_GRID_ROWS = 8
BLOCK_GRID_COLUMNS = 1024
COLUMN_BAND_COUNT = 8
BLOCK_TOTAL = 512
ROWS = 512
COLS = 8192
N_SEC = 8


def set_ends(drawn, key, low, top_value):
    longest = drawn.shape.index(max(drawn.shape))
    spots = []
    for shift in (0, 1):
        where = [jax.random.randint(jax.random.fold_in(key, axis), (), 0, length) for axis, length in enumerate(drawn.shape)]
        where[longest] = (where[longest] + shift) % drawn.shape[longest]
        spots.append(tuple(where))
    return drawn.at[spots[0]].set(low).at[spots[1]].set(top_value)


def levels(key, shape, split, smallest, high):
    def one(position, parts):
        draws = jax.random.uniform(jax.random.fold_in(jax.random.fold_in(key, 6), position), (parts,), jnp.float32, smallest / len(split), high / len(split))
        return jnp.repeat(jnp.exp(draws), shape[position] // parts).reshape((-1,) + (1,) * (len(shape) - position - 1))

    level = one(*split[0])
    for cut in split[1:]:
        level = level * one(*cut)
    return level


def scatter_about(key, shape, width, bound, split=(), dtype=jnp.bfloat16):
    entries = width * jax.random.normal(key, shape, jnp.float32)
    if split:
        entries = entries * levels(key, shape, split, -0.22, 0.18)
    return jnp.clip(entries, -bound, bound).astype(dtype)


def setup_inputs(seed: int = 0) -> dict:
    key_of = jax.random.split(jax.random.key(seed), 6)
    depth = jnp.clip(2.0 * jax.random.uniform(key_of[0], (ROWS, COLS), jnp.float32) ** levels(key_of[0], (ROWS, COLS), ((0, 8), (1, 64)), -0.2, 0.2), 0.0, 2.0)
    elevation = scatter_about(key_of[1], (ROWS, COLS), 1.0, 6.0, ((0, 8), (1, 64)), jnp.float32)
    land_mask = set_ends((jax.random.randint(key_of[2], (ROWS, COLS), 0, 4) < 3).astype(jnp.int32), jax.random.fold_in(key_of[2], 1), 0, 1)
    pressure = scatter_about(key_of[3], (SOIL_LAYER_COUNT, BLOCK_TOTAL, BLOCK_GRID_ROWS, BLOCK_GRID_COLUMNS), 1.0, 6.0, ((1, 512),), jnp.float32)
    saturated_conductance = jnp.clip(jnp.exp(math.log(5.0) - 3.218876 * jax.random.uniform(key_of[4], (SOIL_LAYER_COUNT, BLOCK_TOTAL, BLOCK_GRID_ROWS, BLOCK_GRID_COLUMNS), jnp.float32) ** levels(key_of[4], (SOIL_LAYER_COUNT, BLOCK_TOTAL, BLOCK_GRID_ROWS, BLOCK_GRID_COLUMNS), ((1, 512),), -0.2, 0.2)), 0.2, 5.0)
    return dict(depth=depth, elevation=elevation, land_mask=land_mask, pressure=pressure, saturated_conductance=saturated_conductance)


STORAGE = 0.3
VERTICAL = 2.0
ROUTING = 0.15
LEAKANCE = 0.25
SPECTRUM_MID = 1.025
SPECTRUM_HALF = 0.975


def sweep_factors(number):
    return [1.0 / (SPECTRUM_MID - SPECTRUM_HALF * math.cos(math.pi * (2 * sweep_index + 1) / (2 * number))) for sweep_index in range(number)]


def surface_pair(depth, elevation):
    return jnp.stack([depth + elevation, 1.0 + 0.5 * jnp.tanh(depth)])


def surface_change(padded):
    heads = padded[0]
    mobile = padded[1]
    middle_head = heads[1:-1, 1:-1]
    middle_mobile = mobile[1:-1, 1:-1]
    change = jnp.zeros_like(middle_head)
    others = ((heads[2:, 1:-1], mobile[2:, 1:-1]), (heads[:-2, 1:-1], mobile[:-2, 1:-1]),
              (heads[1:-1, 2:], mobile[1:-1, 2:]), (heads[1:-1, :-2], mobile[1:-1, :-2]))
    for other_head, other_mobile in others:
        change = change + 0.5 * (middle_mobile + other_mobile) * (other_head - middle_head)
    return ROUTING * change


def coefficients(conduct):
    middle = conduct[:, 1:-1, 1:-1]
    row_before = 0.5 * (middle + conduct[:, :-2, 1:-1])
    row_after = 0.5 * (middle + conduct[:, 2:, 1:-1])
    col_before = 0.5 * (middle + conduct[:, 1:-1, :-2])
    col_after = 0.5 * (middle + conduct[:, 1:-1, 2:])
    between = VERTICAL * 0.5 * (middle[:-1] + middle[1:])
    nothing = jnp.zeros_like(middle[:1])
    layer_above = jnp.concatenate([nothing, between], 0)
    layer_below = jnp.concatenate([between, nothing], 0)
    diagonal = STORAGE + row_before + row_after + col_before + col_after + layer_above + layer_below
    return (row_before, row_after, col_before, col_after, layer_above, layer_below, diagonal)


def relaxation(iterate, stencil, right_side, factor):
    row_before, row_after, col_before, col_after, layer_above, layer_below, diagonal = stencil
    middle = iterate[:, 1:-1, 1:-1]
    layers_pad = jnp.pad(middle, ((1, 1), (0, 0), (0, 0)))
    neighbours = (row_before * iterate[:, :-2, 1:-1] + row_after * iterate[:, 2:, 1:-1]
                  + col_before * iterate[:, 1:-1, :-2] + col_after * iterate[:, 1:-1, 2:]
                  + layer_above * layers_pad[:-2] + layer_below * layers_pad[2:])
    return middle + factor * (right_side - diagonal * middle + neighbours) / diagonal


def storage_side(pressure, flux):
    extra = jnp.concatenate([flux[None], jnp.zeros_like(pressure[1:])], 0)
    return STORAGE * pressure + extra


def to_grid(block_layout):
    soil_layers = block_layout.shape[0]
    grid_field = block_layout.reshape(soil_layers, N_SEC, COLUMN_BAND_COUNT, 8, BLOCK_GRID_ROWS, BLOCK_GRID_COLUMNS)
    return grid_field.transpose(0, 1, 3, 4, 2, 5).reshape(soil_layers, ROWS, COLS)


def to_blocks(grid_field):
    soil_layers = grid_field.shape[0]
    block_layout = grid_field.reshape(soil_layers, N_SEC, 8, BLOCK_GRID_ROWS, COLUMN_BAND_COUNT, BLOCK_GRID_COLUMNS)
    return block_layout.transpose(0, 1, 4, 2, 3, 5).reshape(soil_layers, BLOCK_TOTAL, BLOCK_GRID_ROWS, BLOCK_GRID_COLUMNS)


def reference(depth, elevation, land_mask, pressure, saturated_conductance):
    land_share = land_mask.astype(jnp.float32)
    rims = ((0, 0), (1, 1), (1, 1))
    factors = sweep_factors(SWEEPS)
    pressure = to_grid(pressure)
    soil_wide = jnp.pad(to_grid(saturated_conductance), rims)
    for step_number in range(STEPS):
        flux = LEAKANCE * (depth - pressure[0])
        padded = jnp.pad(surface_pair(depth, elevation), rims)
        new_depth = land_share * (depth + surface_change(padded) - flux)
        widened = jnp.pad(pressure, rims)
        stencil = coefficients(soil_wide / (1.0 + widened * widened))
        right_side = storage_side(pressure, flux)
        iterate = relaxation(widened, stencil, right_side, factors[0])
        for factor in factors[1:]:
            iterate = relaxation(jnp.pad(iterate, rims), stencil, right_side, factor)
        depth = new_depth
        pressure = iterate
    return depth, to_blocks(pressure)
```

```python
import math

import jax
import jax.numpy as jnp
from jax import lax
from jax.experimental import pallas as pl
from jax.experimental.pallas import tpu as pltpu
from jax.sharding import Mesh
from jax.sharding import PartitionSpec as P

SWEEPS = 3
STEPS = 4
STORAGE = 0.3
ROUTING = 0.15
LEAKANCE = 0.25
SPECTRUM_MID = 1.025
SPECTRUM_HALF = 0.975

LAYERS = 5
GROUP = 8
HALO = SWEEPS * STEPS
SOIL = 2 * LAYERS
FIELDS = SOIL + 3
SUB = 8
LANES = 128
ROWS = 64
OFF = 24
TALL = OFF + ROWS + 24
STRIP = FIELDS * HALO + 3 * HALO


def sweep_factors(number):
    return [
        1.0
        / (SPECTRUM_MID - SPECTRUM_HALF * math.cos(math.pi * (2 * k + 1) / (2 * number)))
        for k in range(number)
    ]


def lane_index(rows):
    return lax.broadcasted_iota(jnp.int32, (rows, LANES), 1)


def turn(value, shift):
    shift %= LANES
    return pltpu.roll(value, shift, 1) if shift else value


def own_rows(soil, depth, elevation, mask, field, p):
    if field < SOIL:
        return soil[p, field]
    rows = pl.ds(p * SUB, SUB)
    return (depth, elevation, mask)[field - SOIL][rows, :].astype(jnp.float32)


def pack_columns(soil, depth, elevation, mask, left, right):
    lane = lane_index(SUB)
    for p in range(GROUP):
        for plane, fields in ((0, range(SOIL)), (1, range(SOIL, FIELDS))):
            lefts = jnp.zeros((SUB, LANES), jnp.float32)
            rights = jnp.zeros((SUB, LANES), jnp.float32)
            for slot, field in enumerate(fields):
                value = own_rows(soil, depth, elevation, mask, field, p)
                here = (lane >= slot * HALO) & (lane < slot * HALO + HALO)
                lefts = jnp.where(here, turn(value, slot * HALO), lefts)
                rights = jnp.where(here, turn(value, slot * HALO + HALO), rights)
            left[plane, pl.ds(p * SUB, SUB), :] = lefts
            right[plane, pl.ds(p * SUB, SUB), :] = rights


def pack_rows(soil, depth, elevation, mask, from_left, from_right, top, bottom):
    half = HALO - SUB
    for field in range(FIELDS):
        at = field * HALO
        get = lambda p: own_rows(soil, depth, elevation, mask, field, p)
        top[pl.ds(at, SUB), :] = get(0)
        top[pl.ds(at + SUB, half), :] = get(1)[:half]
        bottom[pl.ds(at, half), :] = get(GROUP - 2)[SUB - half :]
        bottom[pl.ds(at + half, SUB), :] = get(GROUP - 1)
    lane = lane_index(HALO)
    for out, first in ((top, 0), (bottom, ROWS - HALO)):
        rows = pl.ds(first, HALO)
        out[pl.ds(FIELDS * HALO, HALO), :] = from_left[0, rows, :]
        out[pl.ds((FIELDS + 1) * HALO, HALO), :] = from_right[0, rows, :]
        out[pl.ds((FIELDS + 2) * HALO, HALO), :] = jnp.where(
            lane < 64, from_left[1, rows, :], turn(from_right[1, rows, :], 64)
        )


def beside(one, two, lane):
    r1, r2 = turn(one, -1), turn(two, -1)
    l1, l2 = turn(one, 1), turn(two, 1)
    last, first = lane == LANES - 1, lane == 0
    right = (jnp.where(last, r2, r1), jnp.where(last, r1, r2))
    left = (jnp.where(first, l2, l1), jnp.where(first, l1, l2))
    return right, left


def march(
    soil, depth_in, elevation_in, mask_in, from_left, from_right, above, below,
    depth_out, pressure_out,
    K, U, X, Y, C, east, west, south, down, inverse, side, D, E, M, H, B,
):
    factors = sweep_factors(SWEEPS)
    zeros = jnp.zeros((SUB, LANES), jnp.float32)
    for plane in range(2):
        for row in (0, TALL - SUB):
            rows = pl.ds(row, SUB)
            for ref in (X, Y, C, south, K, U):
                for layer in range(LAYERS):
                    ref[plane, layer, rows, :] = zeros
            for ref in (D, E, M, H, B):
                ref[plane, rows, :] = zeros
        for row in (SUB, TALL - 2 * SUB):
            rows = pl.ds(row, SUB)
            for ref in (K, U):
                for layer in range(LAYERS):
                    ref[plane, layer, rows, :] = zeros
            for ref in (D, E, M):
                ref[plane, rows, :] = zeros

    def target(field):
        if field < LAYERS:
            return lambda plane, rows: U.at[plane, field, rows, :]
        if field < SOIL:
            return lambda plane, rows: K.at[plane, field - LAYERS, rows, :]
        ref = (D, E, M)[field - SOIL]
        return lambda plane, rows: ref.at[plane, rows, :]

    def spread(lefts, rights, lane, slot, shift=0):
        return jnp.where(
            lane < HALO,
            turn(rights, -slot * HALO - shift),
            jnp.where(lane >= LANES - HALO, turn(lefts, LANES - HALO - slot * HALO), 0.0),
        )

    lane = lane_index(SUB)
    lane_halo = lane_index(HALO)
    for field in range(FIELDS):
        at = target(field)
        slot, plane_in = (field, 0) if field < SOIL else (field - SOIL, 1)
        for p in range(GROUP):
            rows = pl.ds(OFF + p * SUB, SUB)
            at(0, rows)[...] = own_rows(soil, depth_in, elevation_in, mask_in, field, p)
            here = pl.ds(p * SUB, SUB)
            at(1, rows)[...] = spread(
                from_left[plane_in, here, :], from_right[plane_in, here, :], lane, slot
            )
        for packed, first in ((above, OFF - HALO), (below, OFF + ROWS)):
            rows = pl.ds(first, HALO)
            at(0, rows)[...] = packed[pl.ds(field * HALO, HALO), :]
            if field < SOIL:
                lefts = packed[pl.ds(FIELDS * HALO, HALO), :]
                rights = packed[pl.ds((FIELDS + 1) * HALO, HALO), :]
                at(1, rows)[...] = spread(lefts, rights, lane_halo, slot)
            else:
                both = packed[pl.ds((FIELDS + 2) * HALO, HALO), :]
                at(1, rows)[...] = spread(both, both, lane_halo, slot, 64)

    wide = 2 * SUB
    lane2 = lane_index(wide)

    def step(number, carry):
        low = jnp.where(number == 0, SUB, 2 * SUB)
        trips = jnp.where(number == 0, 6, 5)

        def begin(i, carry):
            row = pl.multiple_of(SUB + wide * i, SUB)
            rows = pl.ds(row, wide)
            for plane in range(2):
                depth = D[plane, rows, :]
                H[plane, rows, :] = depth + E[plane, rows, :]
                B[plane, rows, :] = jnp.where(
                    K[plane, 0, rows, :] > 0, 1.0 + 0.5 * jnp.tanh(depth), 0.0
                )
                for layer in range(LAYERS):
                    u = U[plane, layer, rows, :]
                    C[plane, layer, rows, :] = 0.5 * K[plane, layer, rows, :] / (1.0 + u * u)
            return carry

        lax.fori_loop(0, 6, begin, 0)

        def first(i, carry):
            row = pl.multiple_of(low + wide * i, SUB)
            rows, before, after = pl.ds(row, wide), pl.ds(row - 1, wide), pl.ds(row + 1, wide)
            head = [H[plane, rows, :] for plane in range(2)]
            mobile = [B[plane, rows, :] for plane in range(2)]
            head_sides = beside(*head, lane2)
            mobile_sides = beside(*mobile, lane2)
            flux = []
            for plane in range(2):
                depth = D[plane, rows, :]
                now = LEAKANCE * (depth - U[plane, 0, rows, :])
                flux.append(now)
                change = jnp.zeros_like(depth)
                for other_head, other_mobile in (
                    (H[plane, after, :], B[plane, after, :]),
                    (H[plane, before, :], B[plane, before, :]),
                    (head_sides[0][plane], mobile_sides[0][plane]),
                    (head_sides[1][plane], mobile_sides[1][plane]),
                ):
                    change = change + (mobile[plane] + other_mobile) * (other_head - head[plane])
                D[plane, rows, :] = M[plane, rows, :] * (depth + (0.5 * ROUTING) * change - now)
            conduct = [[C[plane, layer, rows, :] for layer in range(LAYERS)] for plane in range(2)]
            iterate = [[U[plane, layer, rows, :] for layer in range(LAYERS)] for plane in range(2)]
            between = [
                [2.0 * (conduct[plane][l] + conduct[plane][l + 1]) for l in range(LAYERS - 1)]
                for plane in range(2)
            ]
            for layer in range(LAYERS):
                c_right, c_left = beside(conduct[0][layer], conduct[1][layer], lane2)
                u_right, u_left = beside(iterate[0][layer], iterate[1][layer], lane2)
                for plane in range(2):
                    c, u = conduct[plane][layer], iterate[plane][layer]
                    e, w = c + c_right[plane], c + c_left[plane]
                    s, n = c + C[plane, layer, after, :], c + C[plane, layer, before, :]
                    diagonal = STORAGE + e + w + s + n
                    total = STORAGE * u
                    if layer == 0:
                        total = total + flux[plane]
                    side[plane, layer, rows, :] = total
                    total = total + e * u_right[plane] + w * u_left[plane]
                    total = total + s * U[plane, layer, after, :] + n * U[plane, layer, before, :]
                    if layer > 0:
                        diagonal = diagonal + between[plane][layer - 1]
                        total = total + between[plane][layer - 1] * iterate[plane][layer - 1]
                    if layer < LAYERS - 1:
                        diagonal = diagonal + between[plane][layer]
                        total = total + between[plane][layer] * iterate[plane][layer + 1]
                        down[plane, layer, rows, :] = between[plane][layer]
                    inv = jnp.where(K[plane, layer, rows, :] > 0, 1.0 / diagonal, 0.0)
                    east[plane, layer, rows, :] = e
                    west[plane, layer, rows, :] = w
                    south[plane, layer, rows, :] = s
                    inverse[plane, layer, rows, :] = inv
                    X[plane, layer, rows, :] = (1.0 - factors[0]) * u + factors[0] * (inv * total)
            return carry

        lax.fori_loop(0, trips, first, 0)

        def sweep(source, goal, factor):
            def body(i, carry):
                row = pl.multiple_of(low + wide * i, SUB)
                rows, before, after = pl.ds(row, wide), pl.ds(row - 1, wide), pl.ds(row + 1, wide)
                iterate = [
                    [source[plane, layer, rows, :] for layer in range(LAYERS)] for plane in range(2)
                ]
                between = [
                    [down[plane, layer, rows, :] for layer in range(LAYERS - 1)]
                    for plane in range(2)
                ]
                for layer in range(LAYERS):
                    u_right, u_left = beside(iterate[0][layer], iterate[1][layer], lane2)
                    for plane in range(2):
                        u = iterate[plane][layer]
                        total = side[plane, layer, rows, :]
                        total = total + east[plane, layer, rows, :] * u_right[plane]
                        total = total + west[plane, layer, rows, :] * u_left[plane]
                        total = total + south[plane, layer, rows, :] * source[plane, layer, after, :]
                        total = total + south[plane, layer, before, :] * source[plane, layer, before, :]
                        if layer > 0:
                            total = total + between[plane][layer - 1] * iterate[plane][layer - 1]
                        if layer < LAYERS - 1:
                            total = total + between[plane][layer] * iterate[plane][layer + 1]
                        inv = inverse[plane, layer, rows, :]
                        goal[plane, layer, rows, :] = (1.0 - factor) * u + factor * (inv * total)
                return carry

            lax.fori_loop(0, trips, body, 0)

        sweep(X, Y, factors[1])
        sweep(Y, U, factors[2])
        return carry

    lax.fori_loop(0, STEPS, step, 0)
    depth_out[...] = D[0, pl.ds(OFF, ROWS), :]
    for p in range(GROUP):
        for layer in range(LAYERS):
            pressure_out[p, layer] = U[0, layer, pl.ds(OFF + p * SUB, SUB), :]


def call(kernel, outs, scratch, *args):
    vmem = pl.BlockSpec(memory_space=pltpu.VMEM)
    return pl.pallas_call(
        kernel,
        out_shape=[jax.ShapeDtypeStruct(shape, jnp.float32) for shape in outs],
        in_specs=[vmem] * len(args),
        out_specs=[vmem] * len(outs),
        scratch_shapes=[pltpu.VMEM(shape, jnp.float32) for shape in scratch],
        compiler_params=pltpu.CompilerParams(vmem_limit_bytes=32 << 20),
    )(*args)


def solution(mesh):
    secs, tiles = mesh.shape["sec"], mesh.shape["tile"]
    axes = ("sec", "band", "place")
    parts = Mesh(mesh.devices.reshape(secs, tiles // GROUP, GROUP), axes)

    def pairs(along, odd):
        found = []
        for s in range(secs):
            for t in range(tiles):
                index, count = (s, secs) if along == "sec" else (t, tiles)
                other = index + 1 if index % 2 == odd else index - 1
                if 0 <= other < count:
                    goal = (other, t) if along == "sec" else (s, other)
                    found.append((s * tiles + t, goal[0] * tiles + goal[1]))
        return found

    def swap(value, along, odd):
        return lax.ppermute(value, axes, pairs(along, odd))

    def local(depth, elevation, land_mask, pressure, conductance):
        tile_odd = lax.axis_index("place") % 2 == 1
        sec_odd = lax.axis_index("sec") % 2 == 1
        blocks = jnp.concatenate([pressure[:, 0], conductance[:, 0]], 0)
        pieces = jnp.moveaxis(blocks.reshape(SOIL, SUB, GROUP, LANES), 2, 0)
        soil = lax.all_to_all(pieces, "place", 0, 0)
        own = (soil, depth, elevation, land_mask)
        left, right = call(pack_columns, [(2, ROWS, LANES)] * 2, [], *own)
        one = swap(jnp.where(tile_odd, left, right), "tile", 0)
        two = swap(jnp.where(tile_odd, right, left), "tile", 1)
        from_left = jnp.where(tile_odd, one, two)
        from_right = jnp.where(tile_odd, two, one)
        top, bottom = call(pack_rows, [(STRIP, LANES)] * 2, [], *own, from_left, from_right)
        one = swap(jnp.where(sec_odd, bottom, top), "sec", 1)
        two = swap(jnp.where(sec_odd, top, bottom), "sec", 0)
        above = jnp.where(sec_odd, two, one)
        below = jnp.where(sec_odd, one, two)
        field, layer = (2, LAYERS, TALL, LANES), (2, TALL, LANES)
        depth, soil = call(
            march,
            [(ROWS, LANES), (GROUP, LAYERS, SUB, LANES)],
            [field] * 11 + [layer] * 5,
            *own, from_left, from_right, above, below,
        )
        soil = lax.all_to_all(soil, "place", 0, 0)
        return depth, jnp.moveaxis(soil, 0, 2).reshape(LAYERS, 1, SUB, GROUP * LANES)

    surface = P("sec", ("band", "place"))
    blocked = P(None, axes, None, None)
    return jax.shard_map(
        local,
        mesh=parts,
        in_specs=(surface, surface, surface, blocked, blocked),
        out_specs=(surface, blocked),
        check_vma=False,
    )
```

```python
import math

import jax
import jax.numpy as jnp
from jax import lax
from jax.experimental import pallas as pl
from jax.experimental.pallas import tpu as pltpu
from jax.sharding import Mesh
from jax.sharding import PartitionSpec as P

SWEEPS = 3
STEPS = 4
STORAGE = 0.3
ROUTING = 0.15
LEAKANCE = 0.25
SPECTRUM_MID = 1.025
SPECTRUM_HALF = 0.975

LAYERS = 5
GROUP = 8
HALO = SWEEPS * STEPS
SOIL = 2 * LAYERS
FIELDS = SOIL + 3
SUB = 8
LANES = 128
ROWS = 64
STRIP = FIELDS * HALO + 3 * HALO


def sweep_factors(number):
    return [
        1.0
        / (SPECTRUM_MID - SPECTRUM_HALF * math.cos(math.pi * (2 * k + 1) / (2 * number)))
        for k in range(number)
    ]


def lane_index(rows):
    return lax.broadcasted_iota(jnp.int32, (rows, LANES), 1)


def turn(value, shift):
    shift %= LANES
    return pltpu.roll(value, shift, 1) if shift else value


def own_rows(soil, depth, elevation, mask, field, p):
    if field < SOIL:
        return soil[p, field]
    rows = pl.ds(p * SUB, SUB)
    return (depth, elevation, mask)[field - SOIL][rows, :].astype(jnp.float32)


def pack_columns(soil, depth, elevation, mask, left, right):
    lane = lane_index(SUB)
    for p in range(GROUP):
        for plane, fields in ((0, range(SOIL)), (1, range(SOIL, FIELDS))):
            lefts = jnp.zeros((SUB, LANES), jnp.float32)
            rights = jnp.zeros((SUB, LANES), jnp.float32)
            for slot, field in enumerate(fields):
                value = own_rows(soil, depth, elevation, mask, field, p)
                here = (lane >= slot * HALO) & (lane < slot * HALO + HALO)
                lefts = jnp.where(here, turn(value, slot * HALO), lefts)
                rights = jnp.where(here, turn(value, slot * HALO + HALO), rights)
            left[plane, pl.ds(p * SUB, SUB), :] = lefts
            right[plane, pl.ds(p * SUB, SUB), :] = rights


def pack_rows(soil, depth, elevation, mask, from_left, from_right, top, bottom):
    half = HALO - SUB
    for field in range(FIELDS):
        at = field * HALO
        get = lambda p: own_rows(soil, depth, elevation, mask, field, p)
        top[pl.ds(at, SUB), :] = get(0)
        top[pl.ds(at + SUB, half), :] = get(1)[:half]
        bottom[pl.ds(at, half), :] = get(GROUP - 2)[SUB - half :]
        bottom[pl.ds(at + half, SUB), :] = get(GROUP - 1)
    lane = lane_index(HALO)
    for out, first in ((top, 0), (bottom, ROWS - HALO)):
        rows = pl.ds(first, HALO)
        out[pl.ds(FIELDS * HALO, HALO), :] = from_left[0, rows, :]
        out[pl.ds((FIELDS + 1) * HALO, HALO), :] = from_right[0, rows, :]
        out[pl.ds((FIELDS + 2) * HALO, HALO), :] = jnp.where(
            lane < 64, from_left[1, rows, :], turn(from_right[1, rows, :], 64)
        )


def beside(one, two, lane):
    r1, r2 = turn(one, -1), turn(two, -1)
    l1, l2 = turn(one, 1), turn(two, 1)
    last, first = lane == LANES - 1, lane == 0
    right = (jnp.where(last, r2, r1), jnp.where(last, r1, r2))
    left = (jnp.where(first, l2, l1), jnp.where(first, l1, l2))
    return right, left


def gather_blocks(pressure, conductance, pieces):
    for j in range(GROUP):
        columns = pl.ds(j * LANES, LANES)
        for layer in range(LAYERS):
            pieces[j, layer] = pressure[layer, 0, :, columns]
            pieces[j, LAYERS + layer] = conductance[layer, 0, :, columns]


def scatter_blocks(pieces, pressure):
    for j in range(GROUP):
        for layer in range(LAYERS):
            pressure[layer, 0, :, pl.ds(j * LANES, LANES)] = pieces[j, layer]


def spread(lefts, rights, lane, slot, shift=0):
    return jnp.where(
        lane < HALO,
        turn(rights, -slot * HALO - shift),
        jnp.where(lane >= LANES - HALO, turn(lefts, LANES - HALO - slot * HALO), 0.0),
    )


PLANES = range(2)


class Field:
    def __init__(self, ref, *where):
        self.ref, self.where = ref, where

    def __getitem__(self, key):
        return self.ref[self.where + key]

    def __setitem__(self, key, value):
        self.ref[self.where + key] = value


def set_conduct(rows, K, U, C, D, E, H, B):
    for plane in PLANES:
        depth = D[plane, rows, :]
        H[plane, rows, :] = depth + E[plane, rows, :]
        B[plane, rows, :] = jnp.where(
            K[plane, 0, rows, :] > 0, 1.0 + 0.5 * jnp.tanh(depth), 0.0
        )
        for layer in range(LAYERS):
            u = U[plane, layer, rows, :]
            C[plane, layer, rows, :] = 0.5 * K[plane, layer, rows, :] / (1.0 + u * u)


def around(row, wide):
    return pl.ds(row, wide), pl.ds(row - 1, wide), pl.ds(row + 1, wide)


def first_sweep(row, wide, at, lane, factor, K, U, X, C, D, M, H, B, faces):
    east, west, south, north, down, inverse, side = faces
    rows, before, after = around(row, wide)
    head = [H[plane, rows, :] for plane in PLANES]
    mobile = [B[plane, rows, :] for plane in PLANES]
    head_sides = beside(*head, lane)
    mobile_sides = beside(*mobile, lane)
    flux = []
    for plane in PLANES:
        depth = D[plane, rows, :]
        now = LEAKANCE * (depth - U[plane, 0, rows, :])
        flux.append(now)
        change = jnp.zeros_like(depth)
        for other_head, other_mobile in (
            (H[plane, after, :], B[plane, after, :]),
            (H[plane, before, :], B[plane, before, :]),
            (head_sides[0][plane], mobile_sides[0][plane]),
            (head_sides[1][plane], mobile_sides[1][plane]),
        ):
            change = change + (mobile[plane] + other_mobile) * (other_head - head[plane])
        D[plane, rows, :] = M[plane, rows, :] * (depth + (0.5 * ROUTING) * change - now)
    conduct = [[C[plane, layer, rows, :] for layer in range(LAYERS)] for plane in PLANES]
    iterate = [[U[plane, layer, rows, :] for layer in range(LAYERS)] for plane in PLANES]
    between = [
        [2.0 * (conduct[plane][l] + conduct[plane][l + 1]) for l in range(LAYERS - 1)]
        for plane in PLANES
    ]
    for layer in range(LAYERS):
        c_right, c_left = beside(conduct[0][layer], conduct[1][layer], lane)
        u_right, u_left = beside(iterate[0][layer], iterate[1][layer], lane)
        for plane in PLANES:
            c, u = conduct[plane][layer], iterate[plane][layer]
            e, w = c + c_right[plane], c + c_left[plane]
            s, n = c + C[plane, layer, after, :], c + C[plane, layer, before, :]
            diagonal = (STORAGE + e) + w + (s + n)
            total = STORAGE * u
            if layer == 0:
                total = total + flux[plane]
            side[plane, layer, at, :] = total
            total = total + e * u_right[plane] + w * u_left[plane]
            total = total + s * U[plane, layer, after, :] + n * U[plane, layer, before, :]
            if layer > 0:
                diagonal = diagonal + between[plane][layer - 1]
                total = total + between[plane][layer - 1] * iterate[plane][layer - 1]
            if layer < LAYERS - 1:
                diagonal = diagonal + between[plane][layer]
                total = total + between[plane][layer] * iterate[plane][layer + 1]
                down[plane, layer, at, :] = between[plane][layer]
            inv = jnp.where(K[plane, layer, rows, :] > 0, 1.0 / diagonal, 0.0)
            east[plane, layer, at, :] = e
            west[plane, layer, at, :] = w
            south[plane, layer, at, :] = s
            north[plane, layer, at, :] = n
            inverse[plane, layer, at, :] = inv
            X[plane, layer, rows, :] = (1.0 - factor) * u + factor * (inv * total)


def later_sweep(row, wide, at, lane, factor, source, goal, faces):
    east, west, south, north, down, inverse, side = faces
    rows, before, after = around(row, wide)
    iterate = [[source[plane, layer, rows, :] for layer in range(LAYERS)] for plane in PLANES]
    between = [[down[plane, layer, at, :] for layer in range(LAYERS - 1)] for plane in PLANES]
    for layer in range(LAYERS):
        u_right, u_left = beside(iterate[0][layer], iterate[1][layer], lane)
        for plane in PLANES:
            u = iterate[plane][layer]
            total = side[plane, layer, at, :]
            total = total + east[plane, layer, at, :] * u_right[plane]
            total = total + west[plane, layer, at, :] * u_left[plane]
            total = total + south[plane, layer, at, :] * source[plane, layer, after, :]
            total = total + north[plane, layer, at, :] * source[plane, layer, before, :]
            if layer > 0:
                total = total + between[plane][layer - 1] * iterate[plane][layer - 1]
            if layer < LAYERS - 1:
                total = total + between[plane][layer] * iterate[plane][layer + 1]
            inv = inverse[plane, layer, at, :]
            goal[plane, layer, rows, :] = (1.0 - factor) * u + factor * (inv * total)


NEAR = 16
TOPS = (SUB, SUB + ROWS - NEAR)
INNER = SUB + ROWS + SUB


def clear(refs, rows):
    for ref in refs:
        lead = ref.shape[:-2]
        value = jnp.zeros((rows.size, LANES), jnp.float32)
        for flat in range(math.prod(lead)):
            where = []
            for size in reversed(lead):
                where.insert(0, flat % size)
                flat //= size
            ref[tuple(where) + (rows, slice(None))] = value


def inner(
    soil, depth_in, elevation_in, mask_in, from_left, from_right,
    depth_out, pressure_out, seen, seen_k, seen_d, seen_e, seen_m,
    K, U, X, Y, C, east, west, south, north, down, inverse, side, D, E, M, H, B,
):
    factors = sweep_factors(SWEEPS)
    faces = (east, west, south, north, down, inverse, side)
    for row in (0, INNER - SUB):
        clear((K, U, X, Y, C, D, E, M, H, B), pl.ds(row, SUB))
    lane = lane_index(SUB)
    for field in range(FIELDS):
        if field < SOIL:
            at, slot, half = Field((U, K)[field // LAYERS]), field, 0
            name = lambda plane, rows: (plane, field % LAYERS, rows, slice(None))
        else:
            at, slot, half = Field((D, E, M)[field - SOIL]), field - SOIL, 1
            name = lambda plane, rows: (plane, rows, slice(None))
        for p in range(GROUP):
            rows, here = pl.ds(SUB + p * SUB, SUB), pl.ds(p * SUB, SUB)
            at[name(0, rows)] = own_rows(soil, depth_in, elevation_in, mask_in, field, p)
            at[name(1, rows)] = spread(
                from_left[half, here, :], from_right[half, here, :], lane, slot
            )

    def note(source, number):
        for edge, top in enumerate(TOPS):
            for plane in PLANES:
                for layer in range(LAYERS):
                    seen[number, edge, plane, layer] = source[plane, layer, pl.ds(top, NEAR), :]

    def note_depth(number):
        for edge, top in enumerate(TOPS):
            for plane in PLANES:
                seen_d[number, edge, plane] = D[plane, pl.ds(top, NEAR), :]

    note(U, 0)
    note_depth(0)
    for edge, top in enumerate(TOPS):
        rows = pl.ds(top, NEAR)
        for plane in PLANES:
            seen_e[edge, plane] = E[plane, rows, :]
            seen_m[edge, plane] = M[plane, rows, :]
            for layer in range(LAYERS):
                seen_k[edge, plane, layer] = K[plane, layer, rows, :]

    wide = 2 * SUB
    lane2 = lane_index(wide)

    def step(number, carry):
        last = number == STEPS - 1
        low = jnp.where(last, 2 * SUB, SUB)
        trips = jnp.where(last, 3, 4)

        def loop(count, begin, body):
            def one(i, carry):
                body(pl.multiple_of(begin + wide * i, SUB))
                return carry

            lax.fori_loop(0, count, one, 0)

        loop(4, SUB, lambda row: set_conduct(pl.ds(row, wide), K, U, C, D, E, H, B))
        loop(
            trips, low,
            lambda row: first_sweep(
                row, wide, pl.ds(row, wide), lane2, factors[0], K, U, X, C, D, M, H, B, faces
            ),
        )
        note(X, 3 * number + 1)
        loop(
            trips, low,
            lambda row: later_sweep(row, wide, pl.ds(row, wide), lane2, factors[1], X, Y, faces),
        )
        note(Y, 3 * number + 2)
        loop(
            trips, low,
            lambda row: later_sweep(row, wide, pl.ds(row, wide), lane2, factors[2], Y, U, faces),
        )

        @pl.when(number < STEPS - 1)
        def _():
            note(U, 3 * number + 3)
            note_depth(number + 1)

        return carry

    lax.fori_loop(0, STEPS, step, 0)
    depth_out[...] = D[0, pl.ds(SUB, ROWS), :]
    for p in range(GROUP):
        for layer in range(LAYERS):
            pressure_out[p, layer] = U[0, layer, pl.ds(SUB + p * SUB, SUB), :]


EDGE = 56


def edges(
    inner_depth, inner_pressure, seen, seen_k, seen_d, seen_e, seen_m, above, below,
    depth_out, pressure_out,
    K, U, X, Y, C, east, west, south, north, down, inverse, side, D, E, M, H, B,
):
    factors = sweep_factors(SWEEPS)
    wide = 2 * SUB
    everything = (K, U, X, Y, D, E, M)
    clear(everything, pl.ds(0, NEAR))
    clear(everything, pl.ds(2 * NEAR, EDGE - 2 * NEAR))
    clear((X, Y), pl.ds(NEAR, NEAR))
    lane = lane_index(HALO)
    own = pl.ds(NEAR, NEAR)
    for edge, (packed, top) in enumerate(((above, NEAR - HALO), (below, 2 * NEAR))):
        rows = pl.ds(top, HALO)
        lefts = packed[pl.ds(FIELDS * HALO, HALO), :]
        rights = packed[pl.ds((FIELDS + 1) * HALO, HALO), :]
        both = packed[pl.ds((FIELDS + 2) * HALO, HALO), :]
        for field in range(FIELDS):
            value = packed[pl.ds(field * HALO, HALO), :]
            if field < SOIL:
                ref, layer = (U, K)[field // LAYERS], field % LAYERS
                ref[edge, 0, layer, rows, :] = value
                ref[edge, 1, layer, rows, :] = spread(lefts, rights, lane, field)
            else:
                ref = (D, E, M)[field - SOIL]
                ref[edge, 0, rows, :] = value
                ref[edge, 1, rows, :] = spread(both, both, lane, field - SOIL, 64)
        for plane in PLANES:
            D[edge, plane, own, :] = seen_d[0, edge, plane]
            E[edge, plane, own, :] = seen_e[edge, plane]
            M[edge, plane, own, :] = seen_m[edge, plane]
            for layer in range(LAYERS):
                U[edge, plane, layer, own, :] = seen[0, edge, plane, layer]
                K[edge, plane, layer, own, :] = seen_k[edge, plane, layer]

    lane2, lane3 = lane_index(wide), lane_index(3 * SUB)
    at = pl.ds(0, wide)

    def step(number, carry):
        starts = (NEAR - 11 + 3 * number, 2 * NEAR - 5 - 3 * number)
        both = range(2)
        of = lambda ref: [Field(ref, edge) for edge in both]
        k, u, x, y, c, d, m, h, b = map(of, (K, U, X, Y, C, D, M, H, B))
        e = of(E)
        faces = [
            [Field(ref, edge) for ref in (east, west, south, north, down, inverse, side)]
            for edge in both
        ]

        def fill(goal, sweep, count):
            for edge in both:
                row = starts[0] + wide if edge == 0 else starts[1] - count
                for plane in PLANES:
                    for layer in range(LAYERS):
                        goal[edge, plane, layer, pl.ds(row, count), :] = seen[
                            sweep, edge, plane, layer, pl.ds(row - NEAR, count), :
                        ]

        for edge in both:
            rows = pl.ds(starts[edge] - 1, 3 * SUB)
            set_conduct(rows, k[edge], u[edge], c[edge], d[edge], e[edge], h[edge], b[edge])
        for edge in both:
            first_sweep(
                starts[edge], wide, at, lane2, factors[0],
                k[edge], u[edge], x[edge], c[edge], d[edge], m[edge], h[edge], b[edge], faces[edge],
            )
        fill(X, 3 * number + 1, 1)
        for edge in both:
            later_sweep(starts[edge], wide, at, lane2, factors[1], x[edge], y[edge], faces[edge])
        fill(Y, 3 * number + 2, 1)
        for edge in both:
            later_sweep(starts[edge], wide, at, lane2, factors[2], y[edge], u[edge], faces[edge])

        @pl.when(number < STEPS - 1)
        def _():
            fill(U, 3 * number + 3, 4)
            for edge in both:
                row = starts[0] + wide if edge == 0 else starts[1] - 4
                for plane in PLANES:
                    D[edge, plane, pl.ds(row, 4), :] = seen_d[
                        number + 1, edge, plane, pl.ds(row - NEAR, 4), :
                    ]

        return carry

    lax.fori_loop(0, STEPS, step, 0)
    left = ROWS - HALO
    depth_out[pl.ds(HALO, ROWS - 2 * HALO), :] = inner_depth[pl.ds(HALO, ROWS - 2 * HALO), :]
    depth_out[pl.ds(0, HALO), :] = D[0, 0, pl.ds(NEAR, HALO), :]
    depth_out[pl.ds(left, HALO), :] = D[1, 0, pl.ds(2 * NEAR - HALO, HALO), :]
    half = HALO - SUB
    for layer in range(LAYERS):
        for p in range(2, GROUP - 2):
            pressure_out[p, layer] = inner_pressure[p, layer]
        pressure_out[0, layer] = U[0, 0, layer, pl.ds(NEAR, SUB), :]
        pressure_out[1, layer, pl.ds(0, half), :] = U[0, 0, layer, pl.ds(NEAR + SUB, half), :]
        pressure_out[1, layer, pl.ds(half, SUB - half), :] = inner_pressure[
            1, layer, pl.ds(half, SUB - half), :
        ]
        pressure_out[GROUP - 2, layer, pl.ds(0, SUB - half), :] = inner_pressure[
            GROUP - 2, layer, pl.ds(0, SUB - half), :
        ]
        pressure_out[GROUP - 2, layer, pl.ds(SUB - half, half), :] = U[
            1, 0, layer, pl.ds(2 * NEAR - HALO, half), :
        ]
        pressure_out[GROUP - 1, layer] = U[1, 0, layer, pl.ds(2 * NEAR - SUB, SUB), :]


def call(kernel, outs, scratch, *args):
    vmem = pl.BlockSpec(memory_space=pltpu.VMEM)
    return pl.pallas_call(
        kernel,
        out_shape=[jax.ShapeDtypeStruct(shape, jnp.float32) for shape in outs],
        in_specs=[vmem] * len(args),
        out_specs=[vmem] * len(outs),
        scratch_shapes=[pltpu.VMEM(shape, jnp.float32) for shape in scratch],
        compiler_params=pltpu.CompilerParams(vmem_limit_bytes=32 << 20),
    )(*args)


def solution(mesh):
    secs, tiles = mesh.shape["sec"], mesh.shape["tile"]
    axes = ("sec", "band", "place")
    parts = Mesh(mesh.devices.reshape(secs, tiles // GROUP, GROUP), axes)

    def pairs(along, odd):
        found = []
        for s in range(secs):
            for t in range(tiles):
                index, count = (s, secs) if along == "sec" else (t, tiles)
                other = index + 1 if index % 2 == odd else index - 1
                if 0 <= other < count:
                    goal = (other, t) if along == "sec" else (s, other)
                    found.append((s * tiles + t, goal[0] * tiles + goal[1]))
        return found

    def swap(value, along, odd):
        return lax.ppermute(value, axes, pairs(along, odd))

    def local(depth, elevation, land_mask, pressure, conductance):
        tile_odd = lax.axis_index("place") % 2 == 1
        sec_odd = lax.axis_index("sec") % 2 == 1
        [pieces] = call(gather_blocks, [(GROUP, SOIL, SUB, LANES)], [], pressure, conductance)
        soil = lax.all_to_all(pieces, "place", 0, 0)
        own = (soil, depth, elevation, land_mask)
        left, right = call(pack_columns, [(2, ROWS, LANES)] * 2, [], *own)
        one = swap(jnp.where(tile_odd, left, right), "tile", 0)
        two = swap(jnp.where(tile_odd, right, left), "tile", 1)
        from_left = jnp.where(tile_odd, one, two)
        from_right = jnp.where(tile_odd, two, one)
        top, bottom = call(pack_rows, [(STRIP, LANES)] * 2, [], *own, from_left, from_right)
        one = swap(jnp.where(sec_odd, bottom, top), "sec", 1)
        two = swap(jnp.where(sec_odd, top, bottom), "sec", 0)
        above = jnp.where(sec_odd, two, one)
        below = jnp.where(sec_odd, one, two)
        near = (2, 2, LAYERS, NEAR, LANES)
        field, layer = (2, LAYERS, INNER, LANES), (2, INNER, LANES)
        shapes = [(ROWS, LANES), (GROUP, LAYERS, SUB, LANES)]
        held = call(
            inner,
            shapes + [(SWEEPS * STEPS,) + near, near, (STEPS, 2, 2, NEAR, LANES)] + [(2, 2, NEAR, LANES)] * 2,
            [field] * 12 + [layer] * 5,
            *own, from_left, from_right,
        )
        field, face, layer = (
            (2, 2, LAYERS, EDGE, LANES),
            (2, 2, LAYERS, 2 * SUB, LANES),
            (2, 2, EDGE, LANES),
        )
        depth, soil = call(
            edges, shapes, [field] * 5 + [face] * 7 + [layer] * 5, *held, above, below
        )
        soil = lax.all_to_all(soil, "place", 0, 0)
        [soil] = call(scatter_blocks, [(LAYERS, 1, SUB, GROUP * LANES)], [], soil)
        return depth, soil

    surface = P("sec", ("band", "place"))
    blocked = P(None, axes, None, None)
    return jax.shard_map(
        local,
        mesh=parts,
        in_specs=(surface, surface, surface, blocked, blocked),
        out_specs=(surface, blocked),
        check_vma=False,
    )
```

```python
import math

import jax
import jax.numpy as jnp
from jax import lax
from jax.experimental import pallas as pl
from jax.experimental.pallas import tpu as pltpu
from jax.sharding import Mesh
from jax.sharding import PartitionSpec as P

SWEEPS = 3
STEPS = 4
STORAGE = 0.3
ROUTING = 0.15
LEAKANCE = 0.25
SPECTRUM_MID = 1.025
SPECTRUM_HALF = 0.975

LAYERS = 5
GROUP = 8
HALO = SWEEPS * STEPS
SOIL = 2 * LAYERS
FIELDS = SOIL + 3
SUB = 8
LANES = 128
ROWS = 64
STRIP = FIELDS * HALO + 3 * HALO


def sweep_factors(number):
    return [
        1.0
        / (SPECTRUM_MID - SPECTRUM_HALF * math.cos(math.pi * (2 * k + 1) / (2 * number)))
        for k in range(number)
    ]


def lane_index(rows):
    return lax.broadcasted_iota(jnp.int32, (rows, LANES), 1)


def turn(value, shift):
    shift %= LANES
    return pltpu.roll(value, shift, 1) if shift else value


def own_rows(soil, surface, field, p):
    if field < SOIL:
        return soil[p, field]
    return surface[field - SOIL, pl.ds(p * SUB, SUB), :]


def pack_columns(soil, surface, left, right):
    lane = lane_index(SUB)
    for p in range(GROUP):
        for plane, fields in ((0, range(SOIL)), (1, range(SOIL, FIELDS))):
            lefts = jnp.zeros((SUB, LANES), jnp.float32)
            rights = jnp.zeros((SUB, LANES), jnp.float32)
            for slot, field in enumerate(fields):
                value = own_rows(soil, surface, field, p)
                here = (lane >= slot * HALO) & (lane < slot * HALO + HALO)
                lefts = jnp.where(here, turn(value, slot * HALO), lefts)
                rights = jnp.where(here, turn(value, slot * HALO + HALO), rights)
            left[plane, pl.ds(p * SUB, SUB), :] = lefts
            right[plane, pl.ds(p * SUB, SUB), :] = rights


def pack_rows(soil, surface, from_left, from_right, top, bottom):
    half = HALO - SUB
    for field in range(FIELDS):
        at = field * HALO
        get = lambda p: own_rows(soil, surface, field, p)
        top[pl.ds(at, SUB), :] = get(0)
        top[pl.ds(at + SUB, half), :] = get(1)[:half]
        bottom[pl.ds(at, half), :] = get(GROUP - 2)[SUB - half :]
        bottom[pl.ds(at + half, SUB), :] = get(GROUP - 1)
    lane = lane_index(HALO)
    for out, first in ((top, 0), (bottom, ROWS - HALO)):
        rows = pl.ds(first, HALO)
        out[pl.ds(FIELDS * HALO, HALO), :] = from_left[0, rows, :]
        out[pl.ds((FIELDS + 1) * HALO, HALO), :] = from_right[0, rows, :]
        out[pl.ds((FIELDS + 2) * HALO, HALO), :] = jnp.where(
            lane < 64, from_left[1, rows, :], turn(from_right[1, rows, :], 64)
        )


def beside(one, two, lane):
    r1, r2 = turn(one, -1), turn(two, -1)
    l1, l2 = turn(one, 1), turn(two, 1)
    last, first = lane == LANES - 1, lane == 0
    right = (jnp.where(last, r2, r1), jnp.where(last, r1, r2))
    left = (jnp.where(first, l2, l1), jnp.where(first, l1, l2))
    return right, left


def gather_blocks(
    pressure, conductance, depth, elevation, mask, pieces, surface, mask_here, sems
):
    copies = [
        pltpu.make_async_copy(
            source.at[:, 0, :, pl.ds(j * LANES, LANES)],
            pieces.at[j, pl.ds(first, LAYERS)],
            sems.at[2 * j + first // LAYERS],
        )
        for j in range(GROUP)
        for source, first in ((pressure, 0), (conductance, LAYERS))
    ]
    count = len(copies)
    copies += [
        pltpu.make_async_copy(source, goal, sems.at[count + i])
        for i, (source, goal) in enumerate(
            ((depth, surface.at[0]), (elevation, surface.at[1]), (mask, mask_here))
        )
    ]
    for copy in copies:
        copy.start()
    for copy in reversed(copies):
        copy.wait()
    surface[2] = mask_here[...].astype(jnp.float32)


def scatter_blocks(pieces, pressure, sems):
    copies = [
        pltpu.make_async_copy(
            pieces.at[j], pressure.at[:, 0, :, pl.ds(j * LANES, LANES)], sems.at[j]
        )
        for j in range(GROUP)
    ]
    for copy in copies:
        copy.start()
    for copy in copies:
        copy.wait()


def spread(lefts, rights, lane, slot, shift=0):
    return jnp.where(
        lane < HALO,
        turn(rights, -slot * HALO - shift),
        jnp.where(lane >= LANES - HALO, turn(lefts, LANES - HALO - slot * HALO), 0.0),
    )


PLANES = range(2)


class Field:
    def __init__(self, ref, *where):
        self.ref, self.where = ref, where

    def __getitem__(self, key):
        return self.ref[self.where + key]

    def __setitem__(self, key, value):
        self.ref[self.where + key] = value


def set_conduct(rows, K, U, C, D, E, H, B):
    for plane in PLANES:
        depth = D[plane, rows, :]
        H[plane, rows, :] = depth + E[plane, rows, :]
        B[plane, rows, :] = jnp.where(
            K[plane, 0, rows, :] > 0, 1.0 + 0.5 * jnp.tanh(depth), 0.0
        )
        for layer in range(LAYERS):
            u = U[plane, layer, rows, :]
            C[plane, layer, rows, :] = 0.5 * K[plane, layer, rows, :] / (1.0 + u * u)


def around(row, wide):
    return pl.ds(row, wide), pl.ds(row - 1, wide), pl.ds(row + 1, wide)


def first_sweep(row, wide, at, lane, factor, K, U, X, C, D, M, H, B, faces):
    east, west, south, north, down, inverse, side = faces
    rows, before, after = around(row, wide)
    head = [H[plane, rows, :] for plane in PLANES]
    mobile = [B[plane, rows, :] for plane in PLANES]
    head_sides = beside(*head, lane)
    mobile_sides = beside(*mobile, lane)
    flux = []
    for plane in PLANES:
        depth = D[plane, rows, :]
        now = LEAKANCE * (depth - U[plane, 0, rows, :])
        flux.append(now)
        change = jnp.zeros_like(depth)
        for other_head, other_mobile in (
            (H[plane, after, :], B[plane, after, :]),
            (H[plane, before, :], B[plane, before, :]),
            (head_sides[0][plane], mobile_sides[0][plane]),
            (head_sides[1][plane], mobile_sides[1][plane]),
        ):
            change = change + (mobile[plane] + other_mobile) * (other_head - head[plane])
        D[plane, rows, :] = M[plane, rows, :] * (depth + (0.5 * ROUTING) * change - now)
    conduct = [[C[plane, layer, rows, :] for layer in range(LAYERS)] for plane in PLANES]
    iterate = [[U[plane, layer, rows, :] for layer in range(LAYERS)] for plane in PLANES]
    between = [
        [2.0 * (conduct[plane][l] + conduct[plane][l + 1]) for l in range(LAYERS - 1)]
        for plane in PLANES
    ]
    for layer in range(LAYERS):
        c_right, c_left = beside(conduct[0][layer], conduct[1][layer], lane)
        u_right, u_left = beside(iterate[0][layer], iterate[1][layer], lane)
        for plane in PLANES:
            c, u = conduct[plane][layer], iterate[plane][layer]
            e, w = c + c_right[plane], c + c_left[plane]
            s, n = c + C[plane, layer, after, :], c + C[plane, layer, before, :]
            diagonal = (STORAGE + e) + w + (s + n)
            total = STORAGE * u
            if layer == 0:
                total = total + flux[plane]
            side[plane, layer, at, :] = total
            total = total + e * u_right[plane] + w * u_left[plane]
            total = total + s * U[plane, layer, after, :] + n * U[plane, layer, before, :]
            if layer > 0:
                diagonal = diagonal + between[plane][layer - 1]
                total = total + between[plane][layer - 1] * iterate[plane][layer - 1]
            if layer < LAYERS - 1:
                diagonal = diagonal + between[plane][layer]
                total = total + between[plane][layer] * iterate[plane][layer + 1]
                down[plane, layer, at, :] = between[plane][layer]
            inv = jnp.where(K[plane, layer, rows, :] > 0, 1.0 / diagonal, 0.0)
            east[plane, layer, at, :] = e
            west[plane, layer, at, :] = w
            south[plane, layer, at, :] = s
            north[plane, layer, at, :] = n
            inverse[plane, layer, at, :] = inv
            X[plane, layer, rows, :] = (1.0 - factor) * u + factor * (inv * total)


def later_sweep(row, wide, at, lane, factor, source, goal, faces):
    east, west, south, north, down, inverse, side = faces
    rows, before, after = around(row, wide)
    iterate = [[source[plane, layer, rows, :] for layer in range(LAYERS)] for plane in PLANES]
    between = [[down[plane, layer, at, :] for layer in range(LAYERS - 1)] for plane in PLANES]
    for layer in range(LAYERS):
        u_right, u_left = beside(iterate[0][layer], iterate[1][layer], lane)
        for plane in PLANES:
            u = iterate[plane][layer]
            total = side[plane, layer, at, :]
            total = total + east[plane, layer, at, :] * u_right[plane]
            total = total + west[plane, layer, at, :] * u_left[plane]
            total = total + south[plane, layer, at, :] * source[plane, layer, after, :]
            total = total + north[plane, layer, at, :] * source[plane, layer, before, :]
            if layer > 0:
                total = total + between[plane][layer - 1] * iterate[plane][layer - 1]
            if layer < LAYERS - 1:
                total = total + between[plane][layer] * iterate[plane][layer + 1]
            inv = inverse[plane, layer, at, :]
            goal[plane, layer, rows, :] = (1.0 - factor) * u + factor * (inv * total)


NEAR = 16
TOPS = (SUB, SUB + ROWS - NEAR)
INNER = SUB + ROWS + SUB


def clear(refs, rows):
    for ref in refs:
        lead = ref.shape[:-2]
        value = jnp.zeros((rows.size, LANES), jnp.float32)
        for flat in range(math.prod(lead)):
            where = []
            for size in reversed(lead):
                where.insert(0, flat % size)
                flat //= size
            ref[tuple(where) + (rows, slice(None))] = value


def inner(
    soil, surface, from_left, from_right,
    depth_out, pressure_out, seen, seen_k, seen_d, seen_e, seen_m,
    K, U, X, Y, C, east, west, south, north, down, inverse, side, D, E, M, H, B,
):
    factors = sweep_factors(SWEEPS)
    faces = (east, west, south, north, down, inverse, side)
    for row in (0, INNER - SUB):
        clear((K, U, X, Y, C, D, E, M, H, B), pl.ds(row, SUB))
    lane = lane_index(SUB)
    for field in range(FIELDS):
        if field < SOIL:
            at, slot, half = Field((U, K)[field // LAYERS]), field, 0
            name = lambda plane, rows: (plane, field % LAYERS, rows, slice(None))
        else:
            at, slot, half = Field((D, E, M)[field - SOIL]), field - SOIL, 1
            name = lambda plane, rows: (plane, rows, slice(None))
        for p in range(GROUP):
            rows, here = pl.ds(SUB + p * SUB, SUB), pl.ds(p * SUB, SUB)
            at[name(0, rows)] = own_rows(soil, surface, field, p)
            at[name(1, rows)] = spread(
                from_left[half, here, :], from_right[half, here, :], lane, slot
            )

    def note(source, number):
        for edge, top in enumerate(TOPS):
            for plane in PLANES:
                for layer in range(LAYERS):
                    seen[number, edge, plane, layer] = source[plane, layer, pl.ds(top, NEAR), :]

    def note_depth(number):
        for edge, top in enumerate(TOPS):
            for plane in PLANES:
                seen_d[number, edge, plane] = D[plane, pl.ds(top, NEAR), :]

    note(U, 0)
    note_depth(0)
    for edge, top in enumerate(TOPS):
        rows = pl.ds(top, NEAR)
        for plane in PLANES:
            seen_e[edge, plane] = E[plane, rows, :]
            seen_m[edge, plane] = M[plane, rows, :]
            for layer in range(LAYERS):
                seen_k[edge, plane, layer] = K[plane, layer, rows, :]

    wide = 2 * SUB
    lane2 = lane_index(wide)

    def step(number):
        last = number == STEPS - 1
        low, trips = (2 * SUB, 3) if last else (SUB, 4)

        def loop(count, begin, body):
            for i in range(count):
                body(begin + wide * i)

        loop(4, SUB, lambda row: set_conduct(pl.ds(row, wide), K, U, C, D, E, H, B))
        loop(
            trips, low,
            lambda row: first_sweep(
                row, wide, pl.ds(row, wide), lane2, factors[0], K, U, X, C, D, M, H, B, faces
            ),
        )
        note(X, 3 * number + 1)
        loop(
            trips, low,
            lambda row: later_sweep(row, wide, pl.ds(row, wide), lane2, factors[1], X, Y, faces),
        )
        note(Y, 3 * number + 2)
        loop(
            trips, low,
            lambda row: later_sweep(row, wide, pl.ds(row, wide), lane2, factors[2], Y, U, faces),
        )

        if not last:
            note(U, 3 * number + 3)
            note_depth(number + 1)

    for number in range(STEPS):
        step(number)
    depth_out[...] = D[0, pl.ds(SUB, ROWS), :]
    for p in range(GROUP):
        for layer in range(LAYERS):
            pressure_out[p, layer] = U[0, layer, pl.ds(SUB + p * SUB, SUB), :]


EDGE = 56


def edges(
    inner_depth, inner_pressure, seen, seen_k, seen_d, seen_e, seen_m, above, below,
    depth_out, pressure_out,
    K, U, X, Y, C, east, west, south, north, down, inverse, side, D, E, M, H, B,
):
    factors = sweep_factors(SWEEPS)
    wide = 2 * SUB
    everything = (K, U, X, Y, D, E, M)
    clear(everything, pl.ds(0, NEAR))
    clear(everything, pl.ds(2 * NEAR, EDGE - 2 * NEAR))
    clear((X, Y), pl.ds(NEAR, NEAR))
    lane = lane_index(HALO)
    own = pl.ds(NEAR, NEAR)
    for edge, (packed, top) in enumerate(((above, NEAR - HALO), (below, 2 * NEAR))):
        rows = pl.ds(top, HALO)
        lefts = packed[pl.ds(FIELDS * HALO, HALO), :]
        rights = packed[pl.ds((FIELDS + 1) * HALO, HALO), :]
        both = packed[pl.ds((FIELDS + 2) * HALO, HALO), :]
        for field in range(FIELDS):
            value = packed[pl.ds(field * HALO, HALO), :]
            if field < SOIL:
                ref, layer = (U, K)[field // LAYERS], field % LAYERS
                ref[edge, 0, layer, rows, :] = value
                ref[edge, 1, layer, rows, :] = spread(lefts, rights, lane, field)
            else:
                ref = (D, E, M)[field - SOIL]
                ref[edge, 0, rows, :] = value
                ref[edge, 1, rows, :] = spread(both, both, lane, field - SOIL, 64)
        for plane in PLANES:
            D[edge, plane, own, :] = seen_d[0, edge, plane]
            E[edge, plane, own, :] = seen_e[edge, plane]
            M[edge, plane, own, :] = seen_m[edge, plane]
            for layer in range(LAYERS):
                U[edge, plane, layer, own, :] = seen[0, edge, plane, layer]
                K[edge, plane, layer, own, :] = seen_k[edge, plane, layer]

    lane2, lane3 = lane_index(wide), lane_index(3 * SUB)
    at = pl.ds(0, wide)

    def step(number):
        starts = (NEAR - 11 + 3 * number, 2 * NEAR - 5 - 3 * number)
        both = range(2)
        of = lambda ref: [Field(ref, edge) for edge in both]
        k, u, x, y, c, d, m, h, b = map(of, (K, U, X, Y, C, D, M, H, B))
        e = of(E)
        faces = [
            [Field(ref, edge) for ref in (east, west, south, north, down, inverse, side)]
            for edge in both
        ]

        def fill(goal, sweep, count):
            for edge in both:
                row = starts[0] + wide if edge == 0 else starts[1] - count
                for plane in PLANES:
                    for layer in range(LAYERS):
                        goal[edge, plane, layer, pl.ds(row, count), :] = seen[
                            sweep, edge, plane, layer, pl.ds(row - NEAR, count), :
                        ]

        for edge in both:
            rows = pl.ds(starts[edge] - 1, 3 * SUB)
            set_conduct(rows, k[edge], u[edge], c[edge], d[edge], e[edge], h[edge], b[edge])
        for edge in both:
            first_sweep(
                starts[edge], wide, at, lane2, factors[0],
                k[edge], u[edge], x[edge], c[edge], d[edge], m[edge], h[edge], b[edge], faces[edge],
            )
        fill(X, 3 * number + 1, 1)
        for edge in both:
            later_sweep(starts[edge], wide, at, lane2, factors[1], x[edge], y[edge], faces[edge])
        fill(Y, 3 * number + 2, 1)
        for edge in both:
            later_sweep(starts[edge], wide, at, lane2, factors[2], y[edge], u[edge], faces[edge])

        if number < STEPS - 1:
            fill(U, 3 * number + 3, 4)
            for edge in both:
                row = starts[0] + wide if edge == 0 else starts[1] - 4
                for plane in PLANES:
                    D[edge, plane, pl.ds(row, 4), :] = seen_d[
                        number + 1, edge, plane, pl.ds(row - NEAR, 4), :
                    ]

    for number in range(STEPS):
        step(number)
    left = ROWS - HALO
    depth_out[pl.ds(HALO, ROWS - 2 * HALO), :] = inner_depth[pl.ds(HALO, ROWS - 2 * HALO), :]
    depth_out[pl.ds(0, HALO), :] = D[0, 0, pl.ds(NEAR, HALO), :]
    depth_out[pl.ds(left, HALO), :] = D[1, 0, pl.ds(2 * NEAR - HALO, HALO), :]
    half = HALO - SUB
    for layer in range(LAYERS):
        for p in range(2, GROUP - 2):
            pressure_out[p, layer] = inner_pressure[p, layer]
        pressure_out[0, layer] = U[0, 0, layer, pl.ds(NEAR, SUB), :]
        pressure_out[1, layer, pl.ds(0, half), :] = U[0, 0, layer, pl.ds(NEAR + SUB, half), :]
        pressure_out[1, layer, pl.ds(half, SUB - half), :] = inner_pressure[
            1, layer, pl.ds(half, SUB - half), :
        ]
        pressure_out[GROUP - 2, layer, pl.ds(0, SUB - half), :] = inner_pressure[
            GROUP - 2, layer, pl.ds(0, SUB - half), :
        ]
        pressure_out[GROUP - 2, layer, pl.ds(SUB - half, half), :] = U[
            1, 0, layer, pl.ds(2 * NEAR - HALO, half), :
        ]
        pressure_out[GROUP - 1, layer] = U[1, 0, layer, pl.ds(2 * NEAR - SUB, SUB), :]


def call(kernel, outs, scratch, *args, places=None):
    places = places or [pltpu.VMEM] * (len(args) + len(outs))
    specs = [pl.BlockSpec(memory_space=place) for place in places]
    args = [
        pltpu.with_memory_space_constraint(arg, place) if place == pltpu.HBM else arg
        for arg, place in zip(args, places)
    ]
    return pl.pallas_call(
        kernel,
        out_shape=[jax.ShapeDtypeStruct(shape, jnp.float32) for shape in outs],
        in_specs=specs[: len(args)],
        out_specs=specs[len(args) :],
        scratch_shapes=[
            pltpu.VMEM(shape, jnp.float32) if isinstance(shape, tuple) else shape
            for shape in scratch
        ],
        compiler_params=pltpu.CompilerParams(vmem_limit_bytes=32 << 20),
    )(*args)


def solution(mesh):
    secs, tiles = mesh.shape["sec"], mesh.shape["tile"]
    axes = ("sec", "band", "place")
    parts = Mesh(mesh.devices.reshape(secs, tiles // GROUP, GROUP), axes)

    def pairs(along, odd):
        found = []
        for s in range(secs):
            for t in range(tiles):
                index, count = (s, secs) if along == "sec" else (t, tiles)
                other = index + 1 if index % 2 == odd else index - 1
                if 0 <= other < count:
                    goal = (other, t) if along == "sec" else (s, other)
                    found.append((s * tiles + t, goal[0] * tiles + goal[1]))
        return found

    def swap(value, along, odd):
        return lax.ppermute(value, axes, pairs(along, odd))

    def local(depth, elevation, land_mask, pressure, conductance):
        tile_odd = lax.axis_index("place") % 2 == 1
        sec_odd = lax.axis_index("sec") % 2 == 1
        pieces, surface = call(
            gather_blocks,
            [(GROUP, SOIL, SUB, LANES), (3, ROWS, LANES)],
            [pltpu.VMEM((ROWS, LANES), jnp.int32), pltpu.SemaphoreType.DMA((2 * GROUP + 3,))],
            pressure, conductance, depth, elevation, land_mask,
            places=[pltpu.HBM] * 5 + [pl.ANY, pltpu.VMEM],
        )
        soil = lax.all_to_all(pieces, "place", 0, 0)
        own = (soil, surface)
        left, right = call(pack_columns, [(2, ROWS, LANES)] * 2, [], *own)
        one = swap(jnp.where(tile_odd, left, right), "tile", 0)
        two = swap(jnp.where(tile_odd, right, left), "tile", 1)
        from_left = jnp.where(tile_odd, one, two)
        from_right = jnp.where(tile_odd, two, one)
        top, bottom = call(pack_rows, [(STRIP, LANES)] * 2, [], *own, from_left, from_right)
        one = swap(jnp.where(sec_odd, bottom, top), "sec", 1)
        two = swap(jnp.where(sec_odd, top, bottom), "sec", 0)
        above = jnp.where(sec_odd, two, one)
        below = jnp.where(sec_odd, one, two)
        near = (2, 2, LAYERS, NEAR, LANES)
        field, layer = (2, LAYERS, INNER, LANES), (2, INNER, LANES)
        shapes = [(ROWS, LANES), (GROUP, LAYERS, SUB, LANES)]
        held = call(
            inner,
            shapes + [(SWEEPS * STEPS,) + near, near, (STEPS, 2, 2, NEAR, LANES)] + [(2, 2, NEAR, LANES)] * 2,
            [field] * 12 + [layer] * 5,
            *own, from_left, from_right,
        )
        field, face, layer = (
            (2, 2, LAYERS, EDGE, LANES),
            (2, 2, LAYERS, 2 * SUB, LANES),
            (2, 2, EDGE, LANES),
        )
        depth, soil = call(
            edges, shapes, [field] * 5 + [face] * 7 + [layer] * 5, *held, above, below
        )
        soil = lax.all_to_all(soil, "place", 0, 0)
        [soil] = call(
            scatter_blocks,
            [(LAYERS, 1, SUB, GROUP * LANES)],
            [pltpu.SemaphoreType.DMA((GROUP,))],
            soil,
            places=[pl.ANY, pltpu.HBM],
        )
        return depth, soil

    surface = P("sec", ("band", "place"))
    blocked = P(None, axes, None, None)
    return jax.shard_map(
        local,
        mesh=parts,
        in_specs=(surface, surface, surface, blocked, blocked),
        out_specs=(surface, blocked),
        check_vma=False,
    )
```

```python
import math

import jax
import jax.numpy as jnp
from jax import lax
from jax.experimental import pallas as pl
from jax.experimental.pallas import tpu as pltpu
from jax.sharding import Mesh
from jax.sharding import PartitionSpec as P

SWEEPS = 3
STEPS = 4
STORAGE = 0.3
ROUTING = 0.15
LEAKANCE = 0.25
SPECTRUM_MID = 1.025
SPECTRUM_HALF = 0.975

LAYERS = 5
GROUP = 8
HALO = SWEEPS * STEPS
SOIL = 2 * LAYERS
FIELDS = SOIL + 3
SUB = 8
LANES = 128
ROWS = 64
STRIP = FIELDS * HALO + 3 * HALO


def sweep_factors(number):
    return [
        1.0
        / (SPECTRUM_MID - SPECTRUM_HALF * math.cos(math.pi * (2 * k + 1) / (2 * number)))
        for k in range(number)
    ]


def lane_index(rows):
    return lax.broadcasted_iota(jnp.int32, (rows, LANES), 1)


def turn(value, shift):
    shift %= LANES
    return pltpu.roll(value, shift, 1) if shift else value


def own_rows(soil, surface, field, p):
    if field < SOIL:
        return soil[p, field]
    return surface[field - SOIL, pl.ds(p * SUB, SUB), :]


def pack_columns(soil, surface, left, right):
    lane = lane_index(SUB)
    for p in range(GROUP):
        for plane, fields in ((0, range(SOIL)), (1, range(SOIL, FIELDS))):
            lefts = jnp.zeros((SUB, LANES), jnp.float32)
            rights = jnp.zeros((SUB, LANES), jnp.float32)
            for slot, field in enumerate(fields):
                value = own_rows(soil, surface, field, p)
                here = (lane >= slot * HALO) & (lane < slot * HALO + HALO)
                lefts = jnp.where(here, turn(value, slot * HALO), lefts)
                rights = jnp.where(here, turn(value, slot * HALO + HALO), rights)
            left[plane, pl.ds(p * SUB, SUB), :] = lefts
            right[plane, pl.ds(p * SUB, SUB), :] = rights


def pack_rows(soil, surface, from_left, from_right, top, bottom):
    half = HALO - SUB
    for field in range(FIELDS):
        at = field * HALO
        get = lambda p: own_rows(soil, surface, field, p)
        top[pl.ds(at, SUB), :] = get(0)
        top[pl.ds(at + SUB, half), :] = get(1)[:half]
        bottom[pl.ds(at, half), :] = get(GROUP - 2)[SUB - half :]
        bottom[pl.ds(at + half, SUB), :] = get(GROUP - 1)
    lane = lane_index(HALO)
    for out, first in ((top, 0), (bottom, ROWS - HALO)):
        rows = pl.ds(first, HALO)
        out[pl.ds(FIELDS * HALO, HALO), :] = from_left[0, rows, :]
        out[pl.ds((FIELDS + 1) * HALO, HALO), :] = from_right[0, rows, :]
        out[pl.ds((FIELDS + 2) * HALO, HALO), :] = jnp.where(
            lane < 64, from_left[1, rows, :], turn(from_right[1, rows, :], 64)
        )


def beside(one, two, lane):
    r1, r2 = turn(one, -1), turn(two, -1)
    l1, l2 = turn(one, 1), turn(two, 1)
    last, first = lane == LANES - 1, lane == 0
    right = (jnp.where(last, r2, r1), jnp.where(last, r1, r2))
    left = (jnp.where(first, l2, l1), jnp.where(first, l1, l2))
    return right, left


def gather_blocks(
    pressure, conductance, depth, elevation, mask, pieces, surface, soil_here, mask_here, sems, sent
):
    arriving = [
        pltpu.make_async_copy(source, goal, sems.at[i])
        for i, (source, goal) in enumerate(
            (
                (pressure.at[:, 0], soil_here.at[0]),
                (conductance.at[:, 0], soil_here.at[1]),
                (depth, surface.at[0]),
                (elevation, surface.at[1]),
                (mask, mask_here),
            )
        )
    ]
    for copy in arriving:
        copy.start()
    leaving = []
    for half in range(2):
        arriving[half].wait()
        for j in range(GROUP):
            copy = pltpu.make_async_copy(
                soil_here.at[half, :, :, pl.ds(j * LANES, LANES)],
                pieces.at[j, pl.ds(half * LAYERS, LAYERS)],
                sent.at[half * GROUP + j],
            )
            copy.start()
            leaving.append(copy)
    for copy in arriving[2:]:
        copy.wait()
    surface[2] = mask_here[...].astype(jnp.float32)
    for copy in leaving:
        copy.wait()


def scatter_blocks(pieces, pressure, sems):
    copies = [
        pltpu.make_async_copy(
            pieces.at[j], pressure.at[:, 0, :, pl.ds(j * LANES, LANES)], sems.at[j]
        )
        for j in range(GROUP)
    ]
    for copy in copies:
        copy.start()
    for copy in copies:
        copy.wait()


def spread(lefts, rights, lane, slot, shift=0):
    return jnp.where(
        lane < HALO,
        turn(rights, -slot * HALO - shift),
        jnp.where(lane >= LANES - HALO, turn(lefts, LANES - HALO - slot * HALO), 0.0),
    )


PLANES = range(2)


class Field:
    def __init__(self, ref, *where):
        self.ref, self.where = ref, where

    def __getitem__(self, key):
        return self.ref[self.where + key]

    def __setitem__(self, key, value):
        self.ref[self.where + key] = value


def set_conduct(rows, K, U, C, D, E, H, B):
    for plane in PLANES:
        depth = D[plane, rows, :]
        H[plane, rows, :] = depth + E[plane, rows, :]
        B[plane, rows, :] = jnp.where(
            K[plane, 0, rows, :] > 0, 1.0 + 0.5 * jnp.tanh(depth), 0.0
        )
        for layer in range(LAYERS):
            u = U[plane, layer, rows, :]
            C[plane, layer, rows, :] = 0.5 * K[plane, layer, rows, :] / (1.0 + u * u)


def around(row, wide):
    return pl.ds(row, wide), pl.ds(row - 1, wide), pl.ds(row + 1, wide)


def first_sweep(row, wide, at, lane, factor, K, U, X, C, D, M, H, B, faces):
    east, west, south, north, down, inverse, side = faces
    rows, before, after = around(row, wide)
    head = [H[plane, rows, :] for plane in PLANES]
    mobile = [B[plane, rows, :] for plane in PLANES]
    head_sides = beside(*head, lane)
    mobile_sides = beside(*mobile, lane)
    flux = []
    for plane in PLANES:
        depth = D[plane, rows, :]
        now = LEAKANCE * (depth - U[plane, 0, rows, :])
        flux.append(now)
        change = jnp.zeros_like(depth)
        for other_head, other_mobile in (
            (H[plane, after, :], B[plane, after, :]),
            (H[plane, before, :], B[plane, before, :]),
            (head_sides[0][plane], mobile_sides[0][plane]),
            (head_sides[1][plane], mobile_sides[1][plane]),
        ):
            change = change + (mobile[plane] + other_mobile) * (other_head - head[plane])
        D[plane, rows, :] = M[plane, rows, :] * (depth + (0.5 * ROUTING) * change - now)
    conduct = [[C[plane, layer, rows, :] for layer in range(LAYERS)] for plane in PLANES]
    iterate = [[U[plane, layer, rows, :] for layer in range(LAYERS)] for plane in PLANES]
    between = [
        [2.0 * (conduct[plane][l] + conduct[plane][l + 1]) for l in range(LAYERS - 1)]
        for plane in PLANES
    ]
    for layer in range(LAYERS):
        c_right, c_left = beside(conduct[0][layer], conduct[1][layer], lane)
        u_right, u_left = beside(iterate[0][layer], iterate[1][layer], lane)
        for plane in PLANES:
            c, u = conduct[plane][layer], iterate[plane][layer]
            e, w = c + c_right[plane], c + c_left[plane]
            s, n = c + C[plane, layer, after, :], c + C[plane, layer, before, :]
            diagonal = (STORAGE + e) + w + (s + n)
            total = STORAGE * u
            if layer == 0:
                total = total + flux[plane]
            side[plane, layer, at, :] = total
            total = total + e * u_right[plane] + w * u_left[plane]
            total = total + s * U[plane, layer, after, :] + n * U[plane, layer, before, :]
            if layer > 0:
                diagonal = diagonal + between[plane][layer - 1]
                total = total + between[plane][layer - 1] * iterate[plane][layer - 1]
            if layer < LAYERS - 1:
                diagonal = diagonal + between[plane][layer]
                total = total + between[plane][layer] * iterate[plane][layer + 1]
                down[plane, layer, at, :] = between[plane][layer]
            inv = jnp.where(K[plane, layer, rows, :] > 0, 1.0 / diagonal, 0.0)
            east[plane, layer, at, :] = e
            west[plane, layer, at, :] = w
            south[plane, layer, at, :] = s
            north[plane, layer, at, :] = n
            inverse[plane, layer, at, :] = inv
            X[plane, layer, rows, :] = (1.0 - factor) * u + factor * (inv * total)


def later_sweep(row, wide, at, lane, factor, source, goal, faces):
    east, west, south, north, down, inverse, side = faces
    rows, before, after = around(row, wide)
    iterate = [[source[plane, layer, rows, :] for layer in range(LAYERS)] for plane in PLANES]
    between = [[down[plane, layer, at, :] for layer in range(LAYERS - 1)] for plane in PLANES]
    for layer in range(LAYERS):
        u_right, u_left = beside(iterate[0][layer], iterate[1][layer], lane)
        for plane in PLANES:
            u = iterate[plane][layer]
            total = side[plane, layer, at, :]
            total = total + east[plane, layer, at, :] * u_right[plane]
            total = total + west[plane, layer, at, :] * u_left[plane]
            total = total + south[plane, layer, at, :] * source[plane, layer, after, :]
            total = total + north[plane, layer, at, :] * source[plane, layer, before, :]
            if layer > 0:
                total = total + between[plane][layer - 1] * iterate[plane][layer - 1]
            if layer < LAYERS - 1:
                total = total + between[plane][layer] * iterate[plane][layer + 1]
            inv = inverse[plane, layer, at, :]
            goal[plane, layer, rows, :] = (1.0 - factor) * u + factor * (inv * total)


NEAR = 16
TOPS = (SUB, SUB + ROWS - NEAR)
INNER = SUB + ROWS + SUB


def clear(refs, rows):
    for ref in refs:
        lead = ref.shape[:-2]
        value = jnp.zeros((rows.size, LANES), jnp.float32)
        for flat in range(math.prod(lead)):
            where = []
            for size in reversed(lead):
                where.insert(0, flat % size)
                flat //= size
            ref[tuple(where) + (rows, slice(None))] = value


def inner(
    soil, surface, from_left, from_right,
    depth_out, pressure_out, seen, seen_k, seen_d, seen_e, seen_m,
    K, U, X, Y, C, east, west, south, north, down, inverse, side, D, E, M, H, B,
):
    factors = sweep_factors(SWEEPS)
    faces = (east, west, south, north, down, inverse, side)
    for row in (0, INNER - SUB):
        clear((K, U, X, Y, C, D, E, M, H, B), pl.ds(row, SUB))
    lane = lane_index(SUB)
    for field in range(FIELDS):
        if field < SOIL:
            at, slot, half = Field((U, K)[field // LAYERS]), field, 0
            name = lambda plane, rows: (plane, field % LAYERS, rows, slice(None))
        else:
            at, slot, half = Field((D, E, M)[field - SOIL]), field - SOIL, 1
            name = lambda plane, rows: (plane, rows, slice(None))
        for p in range(GROUP):
            rows, here = pl.ds(SUB + p * SUB, SUB), pl.ds(p * SUB, SUB)
            at[name(0, rows)] = own_rows(soil, surface, field, p)
            at[name(1, rows)] = spread(
                from_left[half, here, :], from_right[half, here, :], lane, slot
            )

    def note(source, number):
        for edge, top in enumerate(TOPS):
            for plane in PLANES:
                for layer in range(LAYERS):
                    seen[number, edge, plane, layer] = source[plane, layer, pl.ds(top, NEAR), :]

    def note_depth(number):
        for edge, top in enumerate(TOPS):
            for plane in PLANES:
                seen_d[number, edge, plane] = D[plane, pl.ds(top, NEAR), :]

    note(U, 0)
    note_depth(0)
    for edge, top in enumerate(TOPS):
        rows = pl.ds(top, NEAR)
        for plane in PLANES:
            seen_e[edge, plane] = E[plane, rows, :]
            seen_m[edge, plane] = M[plane, rows, :]
            for layer in range(LAYERS):
                seen_k[edge, plane, layer] = K[plane, layer, rows, :]

    wide = 2 * SUB
    lane2 = lane_index(wide)

    def step(number):
        last = number == STEPS - 1
        low, trips = (2 * SUB, 3) if last else (SUB, 4)

        def loop(count, begin, body):
            for i in range(count):
                body(begin + wide * i)

        loop(4, SUB, lambda row: set_conduct(pl.ds(row, wide), K, U, C, D, E, H, B))
        loop(
            trips, low,
            lambda row: first_sweep(
                row, wide, pl.ds(row, wide), lane2, factors[0], K, U, X, C, D, M, H, B, faces
            ),
        )
        note(X, 3 * number + 1)
        loop(
            trips, low,
            lambda row: later_sweep(row, wide, pl.ds(row, wide), lane2, factors[1], X, Y, faces),
        )
        note(Y, 3 * number + 2)
        loop(
            trips, low,
            lambda row: later_sweep(row, wide, pl.ds(row, wide), lane2, factors[2], Y, U, faces),
        )

        if not last:
            note(U, 3 * number + 3)
            note_depth(number + 1)

    for number in range(STEPS):
        step(number)
    depth_out[...] = D[0, pl.ds(SUB, ROWS), :]
    for p in range(GROUP):
        for layer in range(LAYERS):
            pressure_out[p, layer] = U[0, layer, pl.ds(SUB + p * SUB, SUB), :]


EDGE = 56


def edges(
    inner_depth, inner_pressure, seen, seen_k, seen_d, seen_e, seen_m, above, below,
    depth_out, pressure_out,
    K, U, X, Y, C, east, west, south, north, down, inverse, side, D, E, M, H, B,
):
    factors = sweep_factors(SWEEPS)
    wide = 2 * SUB
    everything = (K, U, X, Y, D, E, M)
    clear(everything, pl.ds(0, NEAR))
    clear(everything, pl.ds(2 * NEAR, EDGE - 2 * NEAR))
    clear((X, Y), pl.ds(NEAR, NEAR))
    lane = lane_index(HALO)
    own = pl.ds(NEAR, NEAR)
    for edge, (packed, top) in enumerate(((above, NEAR - HALO), (below, 2 * NEAR))):
        rows = pl.ds(top, HALO)
        lefts = packed[pl.ds(FIELDS * HALO, HALO), :]
        rights = packed[pl.ds((FIELDS + 1) * HALO, HALO), :]
        both = packed[pl.ds((FIELDS + 2) * HALO, HALO), :]
        for field in range(FIELDS):
            value = packed[pl.ds(field * HALO, HALO), :]
            if field < SOIL:
                ref, layer = (U, K)[field // LAYERS], field % LAYERS
                ref[edge, 0, layer, rows, :] = value
                ref[edge, 1, layer, rows, :] = spread(lefts, rights, lane, field)
            else:
                ref = (D, E, M)[field - SOIL]
                ref[edge, 0, rows, :] = value
                ref[edge, 1, rows, :] = spread(both, both, lane, field - SOIL, 64)
        for plane in PLANES:
            D[edge, plane, own, :] = seen_d[0, edge, plane]
            E[edge, plane, own, :] = seen_e[edge, plane]
            M[edge, plane, own, :] = seen_m[edge, plane]
            for layer in range(LAYERS):
                U[edge, plane, layer, own, :] = seen[0, edge, plane, layer]
                K[edge, plane, layer, own, :] = seen_k[edge, plane, layer]

    lane2, lane3 = lane_index(wide), lane_index(3 * SUB)
    at = pl.ds(0, wide)

    def step(number):
        starts = (NEAR - 11 + 3 * number, 2 * NEAR - 5 - 3 * number)
        both = range(2)
        of = lambda ref: [Field(ref, edge) for edge in both]
        k, u, x, y, c, d, m, h, b = map(of, (K, U, X, Y, C, D, M, H, B))
        e = of(E)
        faces = [
            [Field(ref, edge) for ref in (east, west, south, north, down, inverse, side)]
            for edge in both
        ]

        def fill(goal, sweep, count):
            for edge in both:
                row = starts[0] + wide if edge == 0 else starts[1] - count
                for plane in PLANES:
                    for layer in range(LAYERS):
                        goal[edge, plane, layer, pl.ds(row, count), :] = seen[
                            sweep, edge, plane, layer, pl.ds(row - NEAR, count), :
                        ]

        for edge in both:
            rows = pl.ds(starts[edge] - 1, 3 * SUB)
            set_conduct(rows, k[edge], u[edge], c[edge], d[edge], e[edge], h[edge], b[edge])
        for edge in both:
            first_sweep(
                starts[edge], wide, at, lane2, factors[0],
                k[edge], u[edge], x[edge], c[edge], d[edge], m[edge], h[edge], b[edge], faces[edge],
            )
        fill(X, 3 * number + 1, 1)
        for edge in both:
            later_sweep(starts[edge], wide, at, lane2, factors[1], x[edge], y[edge], faces[edge])
        fill(Y, 3 * number + 2, 1)
        for edge in both:
            later_sweep(starts[edge], wide, at, lane2, factors[2], y[edge], u[edge], faces[edge])

        if number < STEPS - 1:
            fill(U, 3 * number + 3, 4)
            for edge in both:
                row = starts[0] + wide if edge == 0 else starts[1] - 4
                for plane in PLANES:
                    D[edge, plane, pl.ds(row, 4), :] = seen_d[
                        number + 1, edge, plane, pl.ds(row - NEAR, 4), :
                    ]

    for number in range(STEPS):
        step(number)
    left = ROWS - HALO
    depth_out[pl.ds(HALO, ROWS - 2 * HALO), :] = inner_depth[pl.ds(HALO, ROWS - 2 * HALO), :]
    depth_out[pl.ds(0, HALO), :] = D[0, 0, pl.ds(NEAR, HALO), :]
    depth_out[pl.ds(left, HALO), :] = D[1, 0, pl.ds(2 * NEAR - HALO, HALO), :]
    half = HALO - SUB
    for layer in range(LAYERS):
        for p in range(2, GROUP - 2):
            pressure_out[p, layer] = inner_pressure[p, layer]
        pressure_out[0, layer] = U[0, 0, layer, pl.ds(NEAR, SUB), :]
        pressure_out[1, layer, pl.ds(0, half), :] = U[0, 0, layer, pl.ds(NEAR + SUB, half), :]
        pressure_out[1, layer, pl.ds(half, SUB - half), :] = inner_pressure[
            1, layer, pl.ds(half, SUB - half), :
        ]
        pressure_out[GROUP - 2, layer, pl.ds(0, SUB - half), :] = inner_pressure[
            GROUP - 2, layer, pl.ds(0, SUB - half), :
        ]
        pressure_out[GROUP - 2, layer, pl.ds(SUB - half, half), :] = U[
            1, 0, layer, pl.ds(2 * NEAR - HALO, half), :
        ]
        pressure_out[GROUP - 1, layer] = U[1, 0, layer, pl.ds(2 * NEAR - SUB, SUB), :]


def call(kernel, outs, scratch, *args, places=None):
    places = places or [pltpu.VMEM] * (len(args) + len(outs))
    specs = [pl.BlockSpec(memory_space=place) for place in places]
    args = [
        pltpu.with_memory_space_constraint(arg, place) if place == pltpu.HBM else arg
        for arg, place in zip(args, places)
    ]
    return pl.pallas_call(
        kernel,
        out_shape=[jax.ShapeDtypeStruct(shape, jnp.float32) for shape in outs],
        in_specs=specs[: len(args)],
        out_specs=specs[len(args) :],
        scratch_shapes=[
            pltpu.VMEM(shape, jnp.float32) if isinstance(shape, tuple) else shape
            for shape in scratch
        ],
        compiler_params=pltpu.CompilerParams(vmem_limit_bytes=32 << 20),
    )(*args)


def solution(mesh):
    secs, tiles = mesh.shape["sec"], mesh.shape["tile"]
    axes = ("sec", "band", "place")
    parts = Mesh(mesh.devices.reshape(secs, tiles // GROUP, GROUP), axes)

    def pairs(along, odd):
        found = []
        for s in range(secs):
            for t in range(tiles):
                index, count = (s, secs) if along == "sec" else (t, tiles)
                other = index + 1 if index % 2 == odd else index - 1
                if 0 <= other < count:
                    goal = (other, t) if along == "sec" else (s, other)
                    found.append((s * tiles + t, goal[0] * tiles + goal[1]))
        return found

    def swap(value, along, odd):
        return lax.ppermute(value, axes, pairs(along, odd))

    def local(depth, elevation, land_mask, pressure, conductance):
        tile_odd = lax.axis_index("place") % 2 == 1
        sec_odd = lax.axis_index("sec") % 2 == 1
        pieces, surface = call(
            gather_blocks,
            [(GROUP, SOIL, SUB, LANES), (3, ROWS, LANES)],
            [
                (2, LAYERS, SUB, GROUP * LANES),
                pltpu.VMEM((ROWS, LANES), jnp.int32),
                pltpu.SemaphoreType.DMA((5,)),
                pltpu.SemaphoreType.DMA((2 * GROUP,)),
            ],
            pressure, conductance, depth, elevation, land_mask,
            places=[pltpu.HBM] * 5 + [pl.ANY, pltpu.VMEM],
        )
        soil = lax.all_to_all(pieces, "place", 0, 0)
        own = (soil, surface)
        left, right = call(pack_columns, [(2, ROWS, LANES)] * 2, [], *own)
        one = swap(jnp.where(tile_odd, left, right), "tile", 0)
        two = swap(jnp.where(tile_odd, right, left), "tile", 1)
        from_left = jnp.where(tile_odd, one, two)
        from_right = jnp.where(tile_odd, two, one)
        top, bottom = call(pack_rows, [(STRIP, LANES)] * 2, [], *own, from_left, from_right)
        one = swap(jnp.where(sec_odd, bottom, top), "sec", 1)
        two = swap(jnp.where(sec_odd, top, bottom), "sec", 0)
        above = jnp.where(sec_odd, two, one)
        below = jnp.where(sec_odd, one, two)
        near = (2, 2, LAYERS, NEAR, LANES)
        field, layer = (2, LAYERS, INNER, LANES), (2, INNER, LANES)
        shapes = [(ROWS, LANES), (GROUP, LAYERS, SUB, LANES)]
        held = call(
            inner,
            shapes + [(SWEEPS * STEPS,) + near, near, (STEPS, 2, 2, NEAR, LANES)] + [(2, 2, NEAR, LANES)] * 2,
            [field] * 12 + [layer] * 5,
            *own, from_left, from_right,
        )
        field, face, layer = (
            (2, 2, LAYERS, EDGE, LANES),
            (2, 2, LAYERS, 2 * SUB, LANES),
            (2, 2, EDGE, LANES),
        )
        depth, soil = call(
            edges, shapes, [field] * 5 + [face] * 7 + [layer] * 5, *held, above, below
        )
        soil = lax.all_to_all(soil, "place", 0, 0)
        [soil] = call(
            scatter_blocks,
            [(LAYERS, 1, SUB, GROUP * LANES)],
            [pltpu.SemaphoreType.DMA((GROUP,))],
            soil,
            places=[pl.ANY, pltpu.HBM],
        )
        return depth, soil

    surface = P("sec", ("band", "place"))
    blocked = P(None, axes, None, None)
    return jax.shard_map(
        local,
        mesh=parts,
        in_specs=(surface, surface, surface, blocked, blocked),
        out_specs=(surface, blocked),
        check_vma=False,
    )
```

```python
import math

import jax
import jax.numpy as jnp
from jax import lax
from jax.experimental import pallas as pl
from jax.experimental.pallas import tpu as pltpu
from jax.sharding import Mesh
from jax.sharding import PartitionSpec as P

SWEEPS = 3
STEPS = 4
STORAGE = 0.3
ROUTING = 0.15
LEAKANCE = 0.25
SPECTRUM_MID = 1.025
SPECTRUM_HALF = 0.975

LAYERS = 5
GROUP = 8
HALO = SWEEPS * STEPS
SOIL = 2 * LAYERS
FIELDS = SOIL + 3
SUB = 8
LANES = 128
ROWS = 64
REACH = (HALO,) * SOIL + (HALO - 1, HALO - SWEEPS, HALO - SWEEPS - 1)
STARTS = tuple(sum(REACH[:field]) for field in range(FIELDS))
CORNERS = sum(REACH)
CORNERS_TOP = CORNERS + HALO
FOLD = 3 * HALO
STRIP = -(-(CORNERS_TOP + HALO // 3) // SUB) * SUB


def sweep_factors(number):
    return [
        1.0
        / (SPECTRUM_MID - SPECTRUM_HALF * math.cos(math.pi * (2 * k + 1) / (2 * number)))
        for k in range(number)
    ]


def lane_index(rows):
    return lax.broadcasted_iota(jnp.int32, (rows, LANES), 1)


def turn(value, shift):
    shift %= LANES
    return pltpu.roll(value, shift, 1) if shift else value


def own_rows(soil, surface, field, p):
    if field < SOIL:
        return soil[p, field]
    return surface[field - SOIL, pl.ds(p * SUB, SUB), :]


def pack_columns(soil, surface, left, right):
    lane = lane_index(SUB)
    for p in range(GROUP):
        for plane, fields in ((0, range(SOIL)), (1, range(SOIL, FIELDS))):
            lefts = jnp.zeros((SUB, LANES), jnp.float32)
            rights = jnp.zeros((SUB, LANES), jnp.float32)
            for slot, field in enumerate(fields):
                value = own_rows(soil, surface, field, p)
                here = (lane >= slot * HALO) & (lane < slot * HALO + HALO)
                lefts = jnp.where(here, turn(value, slot * HALO), lefts)
                rights = jnp.where(here, turn(value, slot * HALO + HALO), rights)
            left[plane, pl.ds(p * SUB, SUB), :] = lefts
            right[plane, pl.ds(p * SUB, SUB), :] = rights


def facing(edge):
    if edge == 0:
        return [(i, HALO - 2 - i, HALO - 1 - i) for i in range(HALO - 1)]
    return [(i, HALO - i, i) for i in range(1, HALO)]


def pack_rows(soil, surface, from_left, from_right, top, bottom, corner):
    lane = lane_index(1)
    column = lane
    for slot in range(1, LANES // HALO + 1):
        column = jnp.where(lane >= slot * HALO, lane - slot * HALO, column)
    for edge, out in enumerate((top, bottom)):
        for field in range(FIELDS):
            at, count = STARTS[field], REACH[field]
            rest = count - SUB
            if edge == 0:
                out[pl.ds(at, SUB), :] = own_rows(soil, surface, field, 0)
                if rest:
                    out[pl.ds(at + SUB, rest), :] = own_rows(soil, surface, field, 1)[:rest]
            else:
                if rest:
                    out[pl.ds(at, rest), :] = own_rows(soil, surface, field, GROUP - 2)[SUB - rest :]
                out[pl.ds(at + rest, SUB), :] = own_rows(soil, surface, field, GROUP - 1)
        first = edge * (ROWS - HALO)
        corner[...] = jnp.zeros((2 * SUB, LANES), jnp.float32)
        out[pl.ds(STRIP - SUB, SUB), :] = jnp.zeros((SUB, LANES), jnp.float32)
        for i, j, right in facing(edge):
            here, there = pl.ds(first + i, 1), pl.ds(first + j, 1)
            take = column < right
            out[pl.ds(CORNERS + i, 1), :] = jnp.where(
                take, from_right[0, here, :], from_left[0, there, :]
            )
            corner[pl.ds(i, 1), :] = jnp.where(
                take, from_right[1, here, :], from_left[1, there, :]
            )
        spare = 0 if edge else HALO - 1
        out[pl.ds(CORNERS + spare, 1), :] = jnp.zeros((1, LANES), jnp.float32)
        some = HALO // 3
        lanes = lane_index(some)
        out[pl.ds(CORNERS_TOP, some), :] = jnp.where(
            lanes < FOLD,
            corner[pl.ds(0, some), :],
            jnp.where(
                lanes < 2 * FOLD,
                turn(corner[pl.ds(some, some), :], FOLD),
                turn(corner[pl.ds(2 * some, some), :], 2 * FOLD),
            ),
        )


def beside(one, two, lane):
    r1, r2 = turn(one, -1), turn(two, -1)
    l1, l2 = turn(one, 1), turn(two, 1)
    last, first = lane == LANES - 1, lane == 0
    right = (jnp.where(last, r2, r1), jnp.where(last, r1, r2))
    left = (jnp.where(first, l2, l1), jnp.where(first, l1, l2))
    return right, left


def gather_blocks(
    pressure, conductance, depth, elevation, mask, pieces, surface, soil_here, mask_here, sems, sent
):
    arriving = [
        pltpu.make_async_copy(source, goal, sems.at[i])
        for i, (source, goal) in enumerate(
            (
                (pressure.at[:, 0], soil_here.at[0]),
                (conductance.at[:, 0], soil_here.at[1]),
                (depth, surface.at[0]),
                (elevation, surface.at[1]),
                (mask, mask_here),
            )
        )
    ]
    for copy in arriving:
        copy.start()
    leaving = []
    for half in range(2):
        arriving[half].wait()
        for j in range(GROUP):
            copy = pltpu.make_async_copy(
                soil_here.at[half, :, :, pl.ds(j * LANES, LANES)],
                pieces.at[j, pl.ds(half * LAYERS, LAYERS)],
                sent.at[half * GROUP + j],
            )
            copy.start()
            leaving.append(copy)
    for copy in arriving[2:]:
        copy.wait()
    surface[2] = mask_here[...].astype(jnp.float32)
    for copy in leaving:
        copy.wait()


def scatter_blocks(pieces, pressure, sems):
    copies = [
        pltpu.make_async_copy(
            pieces.at[j], pressure.at[:, 0, :, pl.ds(j * LANES, LANES)], sems.at[j]
        )
        for j in range(GROUP)
    ]
    for copy in copies:
        copy.start()
    for copy in copies:
        copy.wait()


def spread(lefts, rights, lane, slot):
    return jnp.where(
        lane < HALO,
        turn(rights, -slot * HALO),
        jnp.where(lane >= LANES - HALO, turn(lefts, LANES - HALO - slot * HALO), 0.0),
    )


PLANES = range(2)


class Field:
    def __init__(self, ref, *where):
        self.ref, self.where = ref, where

    def __getitem__(self, key):
        return self.ref[self.where + key]

    def __setitem__(self, key, value):
        self.ref[self.where + key] = value


def set_conduct(rows, K, U, C, D, E, H, B):
    for plane in PLANES:
        depth = D[plane, rows, :]
        H[plane, rows, :] = depth + E[plane, rows, :]
        B[plane, rows, :] = jnp.where(
            K[plane, 0, rows, :] > 0, 1.0 + 0.5 * jnp.tanh(depth), 0.0
        )
        for layer in range(LAYERS):
            u = U[plane, layer, rows, :]
            C[plane, layer, rows, :] = 0.5 * K[plane, layer, rows, :] / (1.0 + u * u)


def around(row, wide):
    return pl.ds(row, wide), pl.ds(row - 1, wide), pl.ds(row + 1, wide)


def first_sweep(row, wide, at, lane, factor, K, U, X, C, D, M, H, B, faces):
    east, west, south, north, down, inverse, side = faces
    rows, before, after = around(row, wide)
    head = [H[plane, rows, :] for plane in PLANES]
    mobile = [B[plane, rows, :] for plane in PLANES]
    head_sides = beside(*head, lane)
    mobile_sides = beside(*mobile, lane)
    flux = []
    for plane in PLANES:
        depth = D[plane, rows, :]
        now = LEAKANCE * (depth - U[plane, 0, rows, :])
        flux.append(now)
        change = jnp.zeros_like(depth)
        for other_head, other_mobile in (
            (H[plane, after, :], B[plane, after, :]),
            (H[plane, before, :], B[plane, before, :]),
            (head_sides[0][plane], mobile_sides[0][plane]),
            (head_sides[1][plane], mobile_sides[1][plane]),
        ):
            change = change + (mobile[plane] + other_mobile) * (other_head - head[plane])
        D[plane, rows, :] = M[plane, rows, :] * (depth + (0.5 * ROUTING) * change - now)
    conduct = [[C[plane, layer, rows, :] for layer in range(LAYERS)] for plane in PLANES]
    iterate = [[U[plane, layer, rows, :] for layer in range(LAYERS)] for plane in PLANES]
    between = [
        [2.0 * (conduct[plane][l] + conduct[plane][l + 1]) for l in range(LAYERS - 1)]
        for plane in PLANES
    ]
    for layer in range(LAYERS):
        c_right, c_left = beside(conduct[0][layer], conduct[1][layer], lane)
        u_right, u_left = beside(iterate[0][layer], iterate[1][layer], lane)
        for plane in PLANES:
            c, u = conduct[plane][layer], iterate[plane][layer]
            e, w = c + c_right[plane], c + c_left[plane]
            s, n = c + C[plane, layer, after, :], c + C[plane, layer, before, :]
            diagonal = (STORAGE + e) + w + (s + n)
            total = STORAGE * u
            if layer == 0:
                total = total + flux[plane]
            side[plane, layer, at, :] = total
            total = total + e * u_right[plane] + w * u_left[plane]
            total = total + s * U[plane, layer, after, :] + n * U[plane, layer, before, :]
            if layer > 0:
                diagonal = diagonal + between[plane][layer - 1]
                total = total + between[plane][layer - 1] * iterate[plane][layer - 1]
            if layer < LAYERS - 1:
                diagonal = diagonal + between[plane][layer]
                total = total + between[plane][layer] * iterate[plane][layer + 1]
                down[plane, layer, at, :] = between[plane][layer]
            inv = jnp.where(K[plane, layer, rows, :] > 0, 1.0 / diagonal, 0.0)
            east[plane, layer, at, :] = e
            west[plane, layer, at, :] = w
            south[plane, layer, at, :] = s
            north[plane, layer, at, :] = n
            inverse[plane, layer, at, :] = inv
            X[plane, layer, rows, :] = (1.0 - factor) * u + factor * (inv * total)


def later_sweep(row, wide, at, lane, factor, source, goal, faces):
    east, west, south, north, down, inverse, side = faces
    rows, before, after = around(row, wide)
    iterate = [[source[plane, layer, rows, :] for layer in range(LAYERS)] for plane in PLANES]
    between = [[down[plane, layer, at, :] for layer in range(LAYERS - 1)] for plane in PLANES]
    for layer in range(LAYERS):
        u_right, u_left = beside(iterate[0][layer], iterate[1][layer], lane)
        for plane in PLANES:
            u = iterate[plane][layer]
            total = side[plane, layer, at, :]
            total = total + east[plane, layer, at, :] * u_right[plane]
            total = total + west[plane, layer, at, :] * u_left[plane]
            total = total + south[plane, layer, at, :] * source[plane, layer, after, :]
            total = total + north[plane, layer, at, :] * source[plane, layer, before, :]
            if layer > 0:
                total = total + between[plane][layer - 1] * iterate[plane][layer - 1]
            if layer < LAYERS - 1:
                total = total + between[plane][layer] * iterate[plane][layer + 1]
            inv = inverse[plane, layer, at, :]
            goal[plane, layer, rows, :] = (1.0 - factor) * u + factor * (inv * total)


NEAR = 16
TOPS = (SUB, SUB + ROWS - NEAR)
INNER = SUB + ROWS + SUB


def clear(refs, rows):
    for ref in refs:
        lead = ref.shape[:-2]
        value = jnp.zeros((rows.size, LANES), jnp.float32)
        for flat in range(math.prod(lead)):
            where = []
            for size in reversed(lead):
                where.insert(0, flat % size)
                flat //= size
            ref[tuple(where) + (rows, slice(None))] = value


def inner(
    soil, surface, from_left, from_right,
    depth_out, pressure_out, seen, seen_k, seen_d, seen_e, seen_m,
    K, U, X, Y, C, east, west, south, north, down, inverse, side, D, E, M, H, B,
):
    factors = sweep_factors(SWEEPS)
    faces = (east, west, south, north, down, inverse, side)
    for row in (0, INNER - SUB):
        clear((K, U, X, Y, C, D, E, M, H, B), pl.ds(row, SUB))
    lane = lane_index(SUB)
    for field in range(FIELDS):
        if field < SOIL:
            at, slot, half = Field((U, K)[field // LAYERS]), field, 0
            name = lambda plane, rows: (plane, field % LAYERS, rows, slice(None))
        else:
            at, slot, half = Field((D, E, M)[field - SOIL]), field - SOIL, 1
            name = lambda plane, rows: (plane, rows, slice(None))
        for p in range(GROUP):
            rows, here = pl.ds(SUB + p * SUB, SUB), pl.ds(p * SUB, SUB)
            at[name(0, rows)] = own_rows(soil, surface, field, p)
            at[name(1, rows)] = spread(
                from_left[half, here, :], from_right[half, here, :], lane, slot
            )

    def note(source, number):
        for edge, top in enumerate(TOPS):
            for plane in PLANES:
                for layer in range(LAYERS):
                    seen[number, edge, plane, layer] = source[plane, layer, pl.ds(top, NEAR), :]

    def note_depth(number):
        for edge, top in enumerate(TOPS):
            for plane in PLANES:
                seen_d[number, edge, plane] = D[plane, pl.ds(top, NEAR), :]

    note(U, 0)
    note_depth(0)
    for edge, top in enumerate(TOPS):
        rows = pl.ds(top, NEAR)
        for plane in PLANES:
            seen_e[edge, plane] = E[plane, rows, :]
            seen_m[edge, plane] = M[plane, rows, :]
            for layer in range(LAYERS):
                seen_k[edge, plane, layer] = K[plane, layer, rows, :]

    wide = 2 * SUB
    lane2 = lane_index(wide)

    def step(number):
        last = number == STEPS - 1
        low, trips = (2 * SUB, 3) if last else (SUB, 4)

        def loop(count, begin, body):
            for i in range(count):
                body(begin + wide * i)

        loop(4, SUB, lambda row: set_conduct(pl.ds(row, wide), K, U, C, D, E, H, B))
        loop(
            trips, low,
            lambda row: first_sweep(
                row, wide, pl.ds(row, wide), lane2, factors[0], K, U, X, C, D, M, H, B, faces
            ),
        )
        note(X, 3 * number + 1)
        loop(
            trips, low,
            lambda row: later_sweep(row, wide, pl.ds(row, wide), lane2, factors[1], X, Y, faces),
        )
        note(Y, 3 * number + 2)
        loop(
            trips, low,
            lambda row: later_sweep(row, wide, pl.ds(row, wide), lane2, factors[2], Y, U, faces),
        )

        if not last:
            note(U, 3 * number + 3)
            note_depth(number + 1)

    for number in range(STEPS):
        step(number)
    depth_out[...] = D[0, pl.ds(SUB, ROWS), :]
    for p in range(GROUP):
        for layer in range(LAYERS):
            pressure_out[p, layer] = U[0, layer, pl.ds(SUB + p * SUB, SUB), :]


EDGE = 56


def edges(
    inner_depth, inner_pressure, seen, seen_k, seen_d, seen_e, seen_m, above, below,
    depth_out, pressure_out,
    K, U, X, Y, C, east, west, south, north, down, inverse, side, D, E, M, H, B, corner,
):
    factors = sweep_factors(SWEEPS)
    wide = 2 * SUB
    everything = (K, U, X, Y, D, E, M)
    clear(everything, pl.ds(0, NEAR))
    clear(everything, pl.ds(2 * NEAR, EDGE - 2 * NEAR))
    clear((X, Y), pl.ds(NEAR, NEAR))
    lane = lane_index(HALO)
    some = HALO // 3
    own = pl.ds(NEAR, NEAR)
    clear((corner,), pl.ds(0, NEAR))
    for edge, packed in enumerate((above, below)):
        for part in range(3):
            corner[edge, 1, pl.ds(part * some, some), :] = turn(
                packed[pl.ds(CORNERS_TOP, some), :], -part * FOLD
            )
        corner[edge, 0, pl.ds(0, HALO), :] = packed[pl.ds(CORNERS, HALO), :]
        for i, j, _ in facing(1 - edge):
            for half in range(2):
                corner[edge, 2 + half, pl.ds(j, 1), :] = corner[edge, half, pl.ds(i, 1), :]
        whole = pl.ds(0, HALO)
        rows = pl.ds(2 * NEAR if edge else NEAR - HALO, HALO)
        for field in range(FIELDS):
            count = REACH[field]
            filled = pl.ds(2 * NEAR if edge else NEAR - count, count)
            value = packed[pl.ds(STARTS[field], count), :]
            half, slot = (0, field) if field < SOIL else (1, field - SOIL)
            sides = spread(
                corner[edge, 2 + half, whole, :], corner[edge, half, whole, :], lane, slot
            )
            if field < SOIL:
                ref, layer = (U, K)[field // LAYERS], field % LAYERS
                ref[edge, 0, layer, filled, :] = value
                ref[edge, 1, layer, rows, :] = sides
            else:
                ref = (D, E, M)[field - SOIL]
                ref[edge, 0, filled, :] = value
                ref[edge, 1, rows, :] = sides
        for plane in PLANES:
            D[edge, plane, own, :] = seen_d[0, edge, plane]
            E[edge, plane, own, :] = seen_e[edge, plane]
            M[edge, plane, own, :] = seen_m[edge, plane]
            for layer in range(LAYERS):
                U[edge, plane, layer, own, :] = seen[0, edge, plane, layer]
                K[edge, plane, layer, own, :] = seen_k[edge, plane, layer]

    lane2, lane3 = lane_index(wide), lane_index(3 * SUB)
    at = pl.ds(0, wide)

    def step(number):
        starts = (NEAR - 11 + 3 * number, 2 * NEAR - 5 - 3 * number)
        both = range(2)
        of = lambda ref: [Field(ref, edge) for edge in both]
        k, u, x, y, c, d, m, h, b = map(of, (K, U, X, Y, C, D, M, H, B))
        e = of(E)
        faces = [
            [Field(ref, edge) for ref in (east, west, south, north, down, inverse, side)]
            for edge in both
        ]

        def fill(goal, sweep, count):
            for edge in both:
                row = starts[0] + wide if edge == 0 else starts[1] - count
                for plane in PLANES:
                    for layer in range(LAYERS):
                        goal[edge, plane, layer, pl.ds(row, count), :] = seen[
                            sweep, edge, plane, layer, pl.ds(row - NEAR, count), :
                        ]

        for edge in both:
            rows = pl.ds(starts[edge] - 1, 3 * SUB)
            set_conduct(rows, k[edge], u[edge], c[edge], d[edge], e[edge], h[edge], b[edge])
        for edge in both:
            first_sweep(
                starts[edge], wide, at, lane2, factors[0],
                k[edge], u[edge], x[edge], c[edge], d[edge], m[edge], h[edge], b[edge], faces[edge],
            )
        fill(X, 3 * number + 1, 1)
        for edge in both:
            later_sweep(starts[edge], wide, at, lane2, factors[1], x[edge], y[edge], faces[edge])
        fill(Y, 3 * number + 2, 1)
        for edge in both:
            later_sweep(starts[edge], wide, at, lane2, factors[2], y[edge], u[edge], faces[edge])

        if number < STEPS - 1:
            fill(U, 3 * number + 3, 4)
            for edge in both:
                row = starts[0] + wide if edge == 0 else starts[1] - 4
                for plane in PLANES:
                    D[edge, plane, pl.ds(row, 4), :] = seen_d[
                        number + 1, edge, plane, pl.ds(row - NEAR, 4), :
                    ]

    for number in range(STEPS):
        step(number)
    left = ROWS - HALO
    depth_out[pl.ds(HALO, ROWS - 2 * HALO), :] = inner_depth[pl.ds(HALO, ROWS - 2 * HALO), :]
    depth_out[pl.ds(0, HALO), :] = D[0, 0, pl.ds(NEAR, HALO), :]
    depth_out[pl.ds(left, HALO), :] = D[1, 0, pl.ds(2 * NEAR - HALO, HALO), :]
    half = HALO - SUB
    for layer in range(LAYERS):
        for p in range(2, GROUP - 2):
            pressure_out[p, layer] = inner_pressure[p, layer]
        pressure_out[0, layer] = U[0, 0, layer, pl.ds(NEAR, SUB), :]
        pressure_out[1, layer, pl.ds(0, half), :] = U[0, 0, layer, pl.ds(NEAR + SUB, half), :]
        pressure_out[1, layer, pl.ds(half, SUB - half), :] = inner_pressure[
            1, layer, pl.ds(half, SUB - half), :
        ]
        pressure_out[GROUP - 2, layer, pl.ds(0, SUB - half), :] = inner_pressure[
            GROUP - 2, layer, pl.ds(0, SUB - half), :
        ]
        pressure_out[GROUP - 2, layer, pl.ds(SUB - half, half), :] = U[
            1, 0, layer, pl.ds(2 * NEAR - HALO, half), :
        ]
        pressure_out[GROUP - 1, layer] = U[1, 0, layer, pl.ds(2 * NEAR - SUB, SUB), :]


def call(kernel, outs, scratch, *args, places=None):
    places = places or [pltpu.VMEM] * (len(args) + len(outs))
    specs = [pl.BlockSpec(memory_space=place) for place in places]
    args = [
        pltpu.with_memory_space_constraint(arg, place) if place == pltpu.HBM else arg
        for arg, place in zip(args, places)
    ]
    return pl.pallas_call(
        kernel,
        out_shape=[jax.ShapeDtypeStruct(shape, jnp.float32) for shape in outs],
        in_specs=specs[: len(args)],
        out_specs=specs[len(args) :],
        scratch_shapes=[
            pltpu.VMEM(shape, jnp.float32) if isinstance(shape, tuple) else shape
            for shape in scratch
        ],
        compiler_params=pltpu.CompilerParams(vmem_limit_bytes=32 << 20),
    )(*args)


def solution(mesh):
    secs, tiles = mesh.shape["sec"], mesh.shape["tile"]
    axes = ("sec", "band", "place")
    parts = Mesh(mesh.devices.reshape(secs, tiles // GROUP, GROUP), axes)

    def pairs(along, odd):
        found = []
        for s in range(secs):
            for t in range(tiles):
                index, count = (s, secs) if along == "sec" else (t, tiles)
                other = index + 1 if index % 2 == odd else index - 1
                if 0 <= other < count:
                    goal = (other, t) if along == "sec" else (s, other)
                    found.append((s * tiles + t, goal[0] * tiles + goal[1]))
        return found

    def swap(value, along, odd):
        return lax.ppermute(value, axes, pairs(along, odd))

    def local(depth, elevation, land_mask, pressure, conductance):
        tile_odd = lax.axis_index("place") % 2 == 1
        sec_odd = lax.axis_index("sec") % 2 == 1
        pieces, surface = call(
            gather_blocks,
            [(GROUP, SOIL, SUB, LANES), (3, ROWS, LANES)],
            [
                (2, LAYERS, SUB, GROUP * LANES),
                pltpu.VMEM((ROWS, LANES), jnp.int32),
                pltpu.SemaphoreType.DMA((5,)),
                pltpu.SemaphoreType.DMA((2 * GROUP,)),
            ],
            pressure, conductance, depth, elevation, land_mask,
            places=[pltpu.HBM] * 5 + [pl.ANY, pltpu.VMEM],
        )
        pieces, tile_odd, sec_odd = lax.optimization_barrier((pieces, tile_odd, sec_odd))
        soil = lax.all_to_all(pieces, "place", 0, 0)
        own = (soil, surface)
        left, right = call(pack_columns, [(2, ROWS, LANES)] * 2, [], *own)
        one = swap(jnp.where(tile_odd, left, right), "tile", 0)
        two = swap(jnp.where(tile_odd, right, left), "tile", 1)
        from_left = jnp.where(tile_odd, one, two)
        from_right = jnp.where(tile_odd, two, one)
        top, bottom = call(
            pack_rows, [(STRIP, LANES)] * 2, [(2 * SUB, LANES)], *own, from_left, from_right
        )
        one = swap(jnp.where(sec_odd, bottom, top), "sec", 1)
        two = swap(jnp.where(sec_odd, top, bottom), "sec", 0)
        above = jnp.where(sec_odd, two, one)
        below = jnp.where(sec_odd, one, two)
        near = (2, 2, LAYERS, NEAR, LANES)
        field, layer = (2, LAYERS, INNER, LANES), (2, INNER, LANES)
        shapes = [(ROWS, LANES), (GROUP, LAYERS, SUB, LANES)]
        held = call(
            inner,
            shapes + [(SWEEPS * STEPS,) + near, near, (STEPS, 2, 2, NEAR, LANES)] + [(2, 2, NEAR, LANES)] * 2,
            [field] * 12 + [layer] * 5,
            *own, from_left, from_right,
        )
        field, face, layer = (
            (2, 2, LAYERS, EDGE, LANES),
            (2, 2, LAYERS, 2 * SUB, LANES),
            (2, 2, EDGE, LANES),
        )
        depth, soil = call(
            edges, shapes, [field] * 5 + [face] * 7 + [layer] * 5 + [(2, 4, NEAR, LANES)], *held, above, below
        )
        soil = lax.all_to_all(soil, "place", 0, 0)
        [soil] = call(
            scatter_blocks,
            [(LAYERS, 1, SUB, GROUP * LANES)],
            [pltpu.SemaphoreType.DMA((GROUP,))],
            soil,
            places=[pl.ANY, pltpu.HBM],
        )
        return depth, soil

    surface = P("sec", ("band", "place"))
    blocked = P(None, axes, None, None)
    return jax.shard_map(
        local,
        mesh=parts,
        in_specs=(surface, surface, surface, blocked, blocked),
        out_specs=(surface, blocked),
        check_vma=False,
    )
```

```python
import math

import jax
import jax.numpy as jnp
from jax import lax
from jax.experimental import pallas as pl
from jax.experimental.pallas import tpu as pltpu
from jax.sharding import Mesh
from jax.sharding import PartitionSpec as P

SWEEPS = 3
STEPS = 4
STORAGE = 0.3
ROUTING = 0.15
LEAKANCE = 0.25
SPECTRUM_MID = 1.025
SPECTRUM_HALF = 0.975

LAYERS = 5
GROUP = 8
HALO = SWEEPS * STEPS
SOIL = 2 * LAYERS
FIELDS = SOIL + 3
SUB = 8
LANES = 128
ROWS = 64
REACH = (HALO,) * SOIL + (HALO - 1, HALO - SWEEPS, HALO - SWEEPS - 1)
STARTS = tuple(sum(REACH[:field]) for field in range(FIELDS))
CORNERS = sum(REACH)
CORNERS_TOP = CORNERS + HALO
FOLD = 3 * HALO
STRIP = -(-(CORNERS_TOP + HALO // 3) // SUB) * SUB


def sweep_factors(number):
    return [
        1.0
        / (SPECTRUM_MID - SPECTRUM_HALF * math.cos(math.pi * (2 * k + 1) / (2 * number)))
        for k in range(number)
    ]


def lane_index(rows):
    return lax.broadcasted_iota(jnp.int32, (rows, LANES), 1)


def turn(value, shift):
    shift %= LANES
    return pltpu.roll(value, shift, 1) if shift else value


def own_rows(soil, surface, field, p):
    if field < SOIL:
        return soil[p, field]
    return surface[field - SOIL, pl.ds(p * SUB, SUB), :]


def edge_columns(values, lane):
    left = right = jnp.zeros(values[0].shape, jnp.float32)
    for slot, value in enumerate(values):
        here = (lane >= slot * HALO) & (lane < slot * HALO + HALO)
        left = jnp.where(here, turn(value, slot * HALO), left)
        right = jnp.where(here, turn(value, slot * HALO + HALO), right)
    return left, right


def pack_columns(soil, left, right):
    lane = lane_index(SUB)
    for p in range(GROUP):
        rows = pl.ds(p * SUB, SUB)
        left[rows, :], right[rows, :] = edge_columns([soil[p, f] for f in range(SOIL)], lane)


def pack_surface(surface, left, right):
    left[...], right[...] = edge_columns([surface[i] for i in range(3)], lane_index(ROWS))


def facing(edge):
    if edge == 0:
        return [(i, HALO - 2 - i, HALO - 1 - i) for i in range(HALO - 1)]
    return [(i, HALO - i, i) for i in range(1, HALO)]


def pack_rows(
    soil, surface, from_left, from_right, over_left, over_right, top, bottom, corner
):
    lane = lane_index(1)
    column = lane
    for slot in range(1, LANES // HALO + 1):
        column = jnp.where(lane >= slot * HALO, lane - slot * HALO, column)
    for edge, out in enumerate((top, bottom)):
        for field in range(FIELDS):
            at, count = STARTS[field], REACH[field]
            rest = count - SUB
            if edge == 0:
                out[pl.ds(at, SUB), :] = own_rows(soil, surface, field, 0)
                if rest:
                    out[pl.ds(at + SUB, rest), :] = own_rows(soil, surface, field, 1)[:rest]
            else:
                if rest:
                    out[pl.ds(at, rest), :] = own_rows(soil, surface, field, GROUP - 2)[SUB - rest :]
                out[pl.ds(at + rest, SUB), :] = own_rows(soil, surface, field, GROUP - 1)
        first = edge * (ROWS - HALO)
        corner[...] = jnp.zeros((2 * SUB, LANES), jnp.float32)
        out[pl.ds(STRIP - SUB, SUB), :] = jnp.zeros((SUB, LANES), jnp.float32)
        for i, j, right in facing(edge):
            here, there = pl.ds(first + i, 1), pl.ds(first + j, 1)
            take = column < right
            out[pl.ds(CORNERS + i, 1), :] = jnp.where(
                take, from_right[here, :], from_left[there, :]
            )
            corner[pl.ds(i, 1), :] = jnp.where(
                take, over_right[here, :], over_left[there, :]
            )
        spare = 0 if edge else HALO - 1
        out[pl.ds(CORNERS + spare, 1), :] = jnp.zeros((1, LANES), jnp.float32)
        some = HALO // 3
        lanes = lane_index(some)
        out[pl.ds(CORNERS_TOP, some), :] = jnp.where(
            lanes < FOLD,
            corner[pl.ds(0, some), :],
            jnp.where(
                lanes < 2 * FOLD,
                turn(corner[pl.ds(some, some), :], FOLD),
                turn(corner[pl.ds(2 * some, some), :], 2 * FOLD),
            ),
        )


def beside(one, two, lane):
    r1, r2 = turn(one, -1), turn(two, -1)
    l1, l2 = turn(one, 1), turn(two, 1)
    last, first = lane == LANES - 1, lane == 0
    right = (jnp.where(last, r2, r1), jnp.where(last, r1, r2))
    left = (jnp.where(first, l2, l1), jnp.where(first, l1, l2))
    return right, left


def gather_blocks(
    pressure, conductance, depth, elevation, mask, pieces, surface, soil_here, band, mask_here, sems, sent
):
    arriving = [
        pltpu.make_async_copy(source, goal, sems.at[i])
        for i, (source, goal) in enumerate(
            (
                (pressure.at[:, 0], soil_here.at[0]),
                (conductance.at[:, 0], soil_here.at[1]),
                (depth, surface.at[0]),
                (elevation, surface.at[1]),
                (mask, mask_here),
            )
        )
    ]
    for copy in arriving:
        copy.start()
    leaving = []
    for half in range(2):
        arriving[half].wait()
        for j in range(GROUP):
            copy = pltpu.make_async_copy(
                soil_here.at[half, :, :, pl.ds(j * LANES, LANES)],
                pieces.at[j, pl.ds(half * LAYERS, LAYERS)],
                sent.at[half * GROUP + j],
            )
            copy.start()
            leaving.append(copy)
    lane = lane_index(SUB)
    ends = [
        edge_columns(
            [
                soil_here[f // LAYERS, f % LAYERS, :, pl.ds(j * LANES, LANES)]
                for f in range(SOIL)
            ],
            lane,
        )
        for j in (0, GROUP - 1)
    ]
    band[0], band[1] = ends[1][1], ends[0][0]
    for j in range(GROUP):
        copy = pltpu.make_async_copy(
            band.at[min(j, 1)], pieces.at[j, SOIL], sent.at[2 * GROUP + j]
        )
        copy.start()
        leaving.append(copy)
    for copy in arriving[2:]:
        copy.wait()
    surface[2] = mask_here[...].astype(jnp.float32)
    for copy in leaving:
        copy.wait()


def scatter_blocks(pieces, pressure, sems):
    copies = [
        pltpu.make_async_copy(
            pieces.at[j], pressure.at[:, 0, :, pl.ds(j * LANES, LANES)], sems.at[j]
        )
        for j in range(GROUP)
    ]
    for copy in copies:
        copy.start()
    for copy in copies:
        copy.wait()


def spread(lefts, rights, lane, slot):
    return jnp.where(
        lane < HALO,
        turn(rights, -slot * HALO),
        jnp.where(lane >= LANES - HALO, turn(lefts, LANES - HALO - slot * HALO), 0.0),
    )


PLANES = range(2)


class Field:
    def __init__(self, ref, *where):
        self.ref, self.where = ref, where

    def __getitem__(self, key):
        return self.ref[self.where + key]

    def __setitem__(self, key, value):
        self.ref[self.where + key] = value


def set_conduct(rows, K, U, C, D, E, H, B):
    for plane in PLANES:
        depth = D[plane, rows, :]
        H[plane, rows, :] = depth + E[plane, rows, :]
        B[plane, rows, :] = jnp.where(
            K[plane, 0, rows, :] > 0, 1.0 + 0.5 * jnp.tanh(depth), 0.0
        )
        for layer in range(LAYERS):
            u = U[plane, layer, rows, :]
            C[plane, layer, rows, :] = 0.5 * K[plane, layer, rows, :] / (1.0 + u * u)


def around(row, wide):
    return pl.ds(row, wide), pl.ds(row - 1, wide), pl.ds(row + 1, wide)


def first_sweep(row, wide, at, lane, factor, K, U, X, C, D, M, H, B, faces):
    east, west, south, north, down, inverse, side = faces
    rows, before, after = around(row, wide)
    head = [H[plane, rows, :] for plane in PLANES]
    mobile = [B[plane, rows, :] for plane in PLANES]
    head_sides = beside(*head, lane)
    mobile_sides = beside(*mobile, lane)
    flux = []
    for plane in PLANES:
        depth = D[plane, rows, :]
        now = LEAKANCE * (depth - U[plane, 0, rows, :])
        flux.append(now)
        change = jnp.zeros_like(depth)
        for other_head, other_mobile in (
            (H[plane, after, :], B[plane, after, :]),
            (H[plane, before, :], B[plane, before, :]),
            (head_sides[0][plane], mobile_sides[0][plane]),
            (head_sides[1][plane], mobile_sides[1][plane]),
        ):
            change = change + (mobile[plane] + other_mobile) * (other_head - head[plane])
        D[plane, rows, :] = M[plane, rows, :] * (depth + (0.5 * ROUTING) * change - now)
    conduct = [[C[plane, layer, rows, :] for layer in range(LAYERS)] for plane in PLANES]
    iterate = [[U[plane, layer, rows, :] for layer in range(LAYERS)] for plane in PLANES]
    between = [
        [2.0 * (conduct[plane][l] + conduct[plane][l + 1]) for l in range(LAYERS - 1)]
        for plane in PLANES
    ]
    for layer in range(LAYERS):
        c_right, c_left = beside(conduct[0][layer], conduct[1][layer], lane)
        u_right, u_left = beside(iterate[0][layer], iterate[1][layer], lane)
        for plane in PLANES:
            c, u = conduct[plane][layer], iterate[plane][layer]
            e, w = c + c_right[plane], c + c_left[plane]
            s, n = c + C[plane, layer, after, :], c + C[plane, layer, before, :]
            diagonal = (STORAGE + e) + w + (s + n)
            total = STORAGE * u
            if layer == 0:
                total = total + flux[plane]
            side[plane, layer, at, :] = total
            total = total + e * u_right[plane] + w * u_left[plane]
            total = total + s * U[plane, layer, after, :] + n * U[plane, layer, before, :]
            if layer > 0:
                diagonal = diagonal + between[plane][layer - 1]
                total = total + between[plane][layer - 1] * iterate[plane][layer - 1]
            if layer < LAYERS - 1:
                diagonal = diagonal + between[plane][layer]
                total = total + between[plane][layer] * iterate[plane][layer + 1]
                down[plane, layer, at, :] = between[plane][layer]
            inv = jnp.where(K[plane, layer, rows, :] > 0, 1.0 / diagonal, 0.0)
            east[plane, layer, at, :] = e
            west[plane, layer, at, :] = w
            south[plane, layer, at, :] = s
            north[plane, layer, at, :] = n
            inverse[plane, layer, at, :] = inv
            X[plane, layer, rows, :] = (1.0 - factor) * u + factor * (inv * total)


def later_sweep(row, wide, at, lane, factor, source, goal, faces):
    east, west, south, north, down, inverse, side = faces
    rows, before, after = around(row, wide)
    iterate = [[source[plane, layer, rows, :] for layer in range(LAYERS)] for plane in PLANES]
    between = [[down[plane, layer, at, :] for layer in range(LAYERS - 1)] for plane in PLANES]
    for layer in range(LAYERS):
        u_right, u_left = beside(iterate[0][layer], iterate[1][layer], lane)
        for plane in PLANES:
            u = iterate[plane][layer]
            total = side[plane, layer, at, :]
            total = total + east[plane, layer, at, :] * u_right[plane]
            total = total + west[plane, layer, at, :] * u_left[plane]
            total = total + south[plane, layer, at, :] * source[plane, layer, after, :]
            total = total + north[plane, layer, at, :] * source[plane, layer, before, :]
            if layer > 0:
                total = total + between[plane][layer - 1] * iterate[plane][layer - 1]
            if layer < LAYERS - 1:
                total = total + between[plane][layer] * iterate[plane][layer + 1]
            inv = inverse[plane, layer, at, :]
            goal[plane, layer, rows, :] = (1.0 - factor) * u + factor * (inv * total)


NEAR = 16
TOPS = (SUB, SUB + ROWS - NEAR)
INNER = SUB + ROWS + SUB


def clear(refs, rows):
    for ref in refs:
        lead = ref.shape[:-2]
        value = jnp.zeros((rows.size, LANES), jnp.float32)
        for flat in range(math.prod(lead)):
            where = []
            for size in reversed(lead):
                where.insert(0, flat % size)
                flat //= size
            ref[tuple(where) + (rows, slice(None))] = value


def inner(
    soil, surface, from_left, from_right, over_left, over_right,
    depth_out, pressure_out, seen, seen_k, seen_d, seen_e, seen_m,
    K, U, X, Y, C, east, west, south, north, down, inverse, side, D, E, M, H, B,
):
    factors = sweep_factors(SWEEPS)
    faces = (east, west, south, north, down, inverse, side)
    for row in (0, INNER - SUB):
        clear((K, U, X, Y, C, D, E, M, H, B), pl.ds(row, SUB))
    lane = lane_index(SUB)
    for field in range(FIELDS):
        if field < SOIL:
            at, slot, half = Field((U, K)[field // LAYERS]), field, 0
            name = lambda plane, rows: (plane, field % LAYERS, rows, slice(None))
        else:
            at, slot, half = Field((D, E, M)[field - SOIL]), field - SOIL, 1
            name = lambda plane, rows: (plane, rows, slice(None))
        for p in range(GROUP):
            rows, here = pl.ds(SUB + p * SUB, SUB), pl.ds(p * SUB, SUB)
            at[name(0, rows)] = own_rows(soil, surface, field, p)
            at[name(1, rows)] = spread(
                (from_left, over_left)[half][here, :],
                (from_right, over_right)[half][here, :],
                lane,
                slot,
            )

    def note(source, number):
        for edge, top in enumerate(TOPS):
            for plane in PLANES:
                for layer in range(LAYERS):
                    seen[number, edge, plane, layer] = source[plane, layer, pl.ds(top, NEAR), :]

    def note_depth(number):
        for edge, top in enumerate(TOPS):
            for plane in PLANES:
                seen_d[number, edge, plane] = D[plane, pl.ds(top, NEAR), :]

    note(U, 0)
    note_depth(0)
    for edge, top in enumerate(TOPS):
        rows = pl.ds(top, NEAR)
        for plane in PLANES:
            seen_e[edge, plane] = E[plane, rows, :]
            seen_m[edge, plane] = M[plane, rows, :]
            for layer in range(LAYERS):
                seen_k[edge, plane, layer] = K[plane, layer, rows, :]

    wide = 2 * SUB
    lane2 = lane_index(wide)

    def step(number):
        last = number == STEPS - 1
        low, trips = (2 * SUB, 3) if last else (SUB, 4)

        def loop(count, begin, body):
            for i in range(count):
                body(begin + wide * i)

        loop(4, SUB, lambda row: set_conduct(pl.ds(row, wide), K, U, C, D, E, H, B))
        loop(
            trips, low,
            lambda row: first_sweep(
                row, wide, pl.ds(row, wide), lane2, factors[0], K, U, X, C, D, M, H, B, faces
            ),
        )
        note(X, 3 * number + 1)
        loop(
            trips, low,
            lambda row: later_sweep(row, wide, pl.ds(row, wide), lane2, factors[1], X, Y, faces),
        )
        note(Y, 3 * number + 2)
        loop(
            trips, low,
            lambda row: later_sweep(row, wide, pl.ds(row, wide), lane2, factors[2], Y, U, faces),
        )

        if not last:
            note(U, 3 * number + 3)
            note_depth(number + 1)

    for number in range(STEPS):
        step(number)
    depth_out[...] = D[0, pl.ds(SUB, ROWS), :]
    for p in range(GROUP):
        for layer in range(LAYERS):
            pressure_out[p, layer] = U[0, layer, pl.ds(SUB + p * SUB, SUB), :]


EDGE = 56


def edges(
    inner_depth, inner_pressure, seen, seen_k, seen_d, seen_e, seen_m, above, below,
    depth_out, pressure_out,
    K, U, X, Y, C, east, west, south, north, down, inverse, side, D, E, M, H, B, corner,
):
    factors = sweep_factors(SWEEPS)
    wide = 2 * SUB
    everything = (K, U, X, Y, D, E, M)
    clear(everything, pl.ds(0, NEAR))
    clear(everything, pl.ds(2 * NEAR, EDGE - 2 * NEAR))
    clear((X, Y), pl.ds(NEAR, NEAR))
    lane = lane_index(HALO)
    some = HALO // 3
    own = pl.ds(NEAR, NEAR)
    clear((corner,), pl.ds(0, NEAR))
    for edge, packed in enumerate((above, below)):
        for part in range(3):
            corner[edge, 1, pl.ds(part * some, some), :] = turn(
                packed[pl.ds(CORNERS_TOP, some), :], -part * FOLD
            )
        corner[edge, 0, pl.ds(0, HALO), :] = packed[pl.ds(CORNERS, HALO), :]
        for i, j, _ in facing(1 - edge):
            for half in range(2):
                corner[edge, 2 + half, pl.ds(j, 1), :] = corner[edge, half, pl.ds(i, 1), :]
        whole = pl.ds(0, HALO)
        rows = pl.ds(2 * NEAR if edge else NEAR - HALO, HALO)
        for field in range(FIELDS):
            count = REACH[field]
            filled = pl.ds(2 * NEAR if edge else NEAR - count, count)
            value = packed[pl.ds(STARTS[field], count), :]
            half, slot = (0, field) if field < SOIL else (1, field - SOIL)
            sides = spread(
                corner[edge, 2 + half, whole, :], corner[edge, half, whole, :], lane, slot
            )
            if field < SOIL:
                ref, layer = (U, K)[field // LAYERS], field % LAYERS
                ref[edge, 0, layer, filled, :] = value
                ref[edge, 1, layer, rows, :] = sides
            else:
                ref = (D, E, M)[field - SOIL]
                ref[edge, 0, filled, :] = value
                ref[edge, 1, rows, :] = sides
        for plane in PLANES:
            D[edge, plane, own, :] = seen_d[0, edge, plane]
            E[edge, plane, own, :] = seen_e[edge, plane]
            M[edge, plane, own, :] = seen_m[edge, plane]
            for layer in range(LAYERS):
                U[edge, plane, layer, own, :] = seen[0, edge, plane, layer]
                K[edge, plane, layer, own, :] = seen_k[edge, plane, layer]

    lane2, lane3 = lane_index(wide), lane_index(3 * SUB)
    at = pl.ds(0, wide)

    def step(number):
        starts = (NEAR - 11 + 3 * number, 2 * NEAR - 5 - 3 * number)
        both = range(2)
        of = lambda ref: [Field(ref, edge) for edge in both]
        k, u, x, y, c, d, m, h, b = map(of, (K, U, X, Y, C, D, M, H, B))
        e = of(E)
        faces = [
            [Field(ref, edge) for ref in (east, west, south, north, down, inverse, side)]
            for edge in both
        ]

        def fill(goal, sweep, count):
            for edge in both:
                row = starts[0] + wide if edge == 0 else starts[1] - count
                for plane in PLANES:
                    for layer in range(LAYERS):
                        goal[edge, plane, layer, pl.ds(row, count), :] = seen[
                            sweep, edge, plane, layer, pl.ds(row - NEAR, count), :
                        ]

        for edge in both:
            rows = pl.ds(starts[edge] - 1, 3 * SUB)
            set_conduct(rows, k[edge], u[edge], c[edge], d[edge], e[edge], h[edge], b[edge])
        for edge in both:
            first_sweep(
                starts[edge], wide, at, lane2, factors[0],
                k[edge], u[edge], x[edge], c[edge], d[edge], m[edge], h[edge], b[edge], faces[edge],
            )
        fill(X, 3 * number + 1, 1)
        for edge in both:
            later_sweep(starts[edge], wide, at, lane2, factors[1], x[edge], y[edge], faces[edge])
        fill(Y, 3 * number + 2, 1)
        for edge in both:
            later_sweep(starts[edge], wide, at, lane2, factors[2], y[edge], u[edge], faces[edge])

        if number < STEPS - 1:
            fill(U, 3 * number + 3, 4)
            for edge in both:
                row = starts[0] + wide if edge == 0 else starts[1] - 4
                for plane in PLANES:
                    D[edge, plane, pl.ds(row, 4), :] = seen_d[
                        number + 1, edge, plane, pl.ds(row - NEAR, 4), :
                    ]

    for number in range(STEPS):
        step(number)
    left = ROWS - HALO
    depth_out[pl.ds(HALO, ROWS - 2 * HALO), :] = inner_depth[pl.ds(HALO, ROWS - 2 * HALO), :]
    depth_out[pl.ds(0, HALO), :] = D[0, 0, pl.ds(NEAR, HALO), :]
    depth_out[pl.ds(left, HALO), :] = D[1, 0, pl.ds(2 * NEAR - HALO, HALO), :]
    half = HALO - SUB
    for layer in range(LAYERS):
        for p in range(2, GROUP - 2):
            pressure_out[p, layer] = inner_pressure[p, layer]
        pressure_out[0, layer] = U[0, 0, layer, pl.ds(NEAR, SUB), :]
        pressure_out[1, layer, pl.ds(0, half), :] = U[0, 0, layer, pl.ds(NEAR + SUB, half), :]
        pressure_out[1, layer, pl.ds(half, SUB - half), :] = inner_pressure[
            1, layer, pl.ds(half, SUB - half), :
        ]
        pressure_out[GROUP - 2, layer, pl.ds(0, SUB - half), :] = inner_pressure[
            GROUP - 2, layer, pl.ds(0, SUB - half), :
        ]
        pressure_out[GROUP - 2, layer, pl.ds(SUB - half, half), :] = U[
            1, 0, layer, pl.ds(2 * NEAR - HALO, half), :
        ]
        pressure_out[GROUP - 1, layer] = U[1, 0, layer, pl.ds(2 * NEAR - SUB, SUB), :]


def call(kernel, outs, scratch, *args, places=None):
    places = places or [pltpu.VMEM] * (len(args) + len(outs))
    specs = [pl.BlockSpec(memory_space=place) for place in places]
    args = [
        pltpu.with_memory_space_constraint(arg, place) if place == pltpu.HBM else arg
        for arg, place in zip(args, places)
    ]
    return pl.pallas_call(
        kernel,
        out_shape=[jax.ShapeDtypeStruct(shape, jnp.float32) for shape in outs],
        in_specs=specs[: len(args)],
        out_specs=specs[len(args) :],
        scratch_shapes=[
            pltpu.VMEM(shape, jnp.float32) if isinstance(shape, tuple) else shape
            for shape in scratch
        ],
        compiler_params=pltpu.CompilerParams(vmem_limit_bytes=32 << 20),
    )(*args)


def solution(mesh):
    secs, tiles = mesh.shape["sec"], mesh.shape["tile"]
    axes = ("sec", "band", "place")
    parts = Mesh(mesh.devices.reshape(secs, tiles // GROUP, GROUP), axes)

    def pairs(along, odd):
        found = []
        for s in range(secs):
            for t in range(tiles):
                index, count = (s, secs) if along == "sec" else (t, tiles)
                other = index + 1 if index % 2 == odd else index - 1
                if 0 <= other < count:
                    goal = (other, t) if along == "sec" else (s, other)
                    found.append((s * tiles + t, goal[0] * tiles + goal[1]))
        return found

    def bands():
        found = [
            (i, j)
            for i, j in pairs("tile", 1)
            if i % tiles // GROUP == j % tiles // GROUP
        ]
        for s in range(secs):
            for t in range(0, tiles - GROUP, GROUP):
                here = s * tiles + t
                found.append((here, here + GROUP))
                found.append((here + 2 * GROUP - 1, here + GROUP - 1))
        return found

    def swap(value, along, odd):
        return lax.ppermute(value, axes, pairs(along, odd))

    def local(depth, elevation, land_mask, pressure, conductance):
        place = lax.axis_index("place")
        tile_odd = place % 2 == 1
        tile_end = (place == 0) | (place == GROUP - 1)
        sec_odd = lax.axis_index("sec") % 2 == 1
        pieces, surface = call(
            gather_blocks,
            [(GROUP, SOIL + 1, SUB, LANES), (3, ROWS, LANES)],
            [
                (2, LAYERS, SUB, GROUP * LANES),
                (2, SUB, LANES),
                pltpu.VMEM((ROWS, LANES), jnp.int32),
                pltpu.SemaphoreType.DMA((5,)),
                pltpu.SemaphoreType.DMA((3 * GROUP,)),
            ],
            pressure, conductance, depth, elevation, land_mask,
            places=[pltpu.HBM] * 5 + [pl.ANY, pltpu.VMEM],
        )
        soil = lax.all_to_all(pieces, "place", 0, 0)
        own = (soil, surface)
        edge = (ROWS, LANES)

        def exchange(left, right, outer, second):
            one = lax.ppermute(jnp.where(tile_odd, left, right), axes, pairs("tile", 0))
            two = jnp.where(tile_odd, right, left)
            if outer is not None:
                two = jnp.where(tile_end, outer, two)
            two = lax.ppermute(two, axes, second)
            return jnp.where(tile_odd, one, two), jnp.where(tile_odd, two, one)

        left, right = call(pack_surface, [edge] * 2, [], surface)
        over = exchange(left, right, None, pairs("tile", 1))
        left, right = call(pack_columns, [edge] * 2, [], soil)
        beyond = exchange(left, right, soil[:, SOIL].reshape(edge), bands())
        halos = (*beyond, *over)
        top, bottom = call(
            pack_rows, [(STRIP, LANES)] * 2, [(2 * SUB, LANES)], *own, *halos
        )
        one = swap(jnp.where(sec_odd, bottom, top), "sec", 1)
        two = swap(jnp.where(sec_odd, top, bottom), "sec", 0)
        above = jnp.where(sec_odd, two, one)
        below = jnp.where(sec_odd, one, two)
        near = (2, 2, LAYERS, NEAR, LANES)
        field, layer = (2, LAYERS, INNER, LANES), (2, INNER, LANES)
        shapes = [(ROWS, LANES), (GROUP, LAYERS, SUB, LANES)]
        held = call(
            inner,
            shapes + [(SWEEPS * STEPS,) + near, near, (STEPS, 2, 2, NEAR, LANES)] + [(2, 2, NEAR, LANES)] * 2,
            [field] * 12 + [layer] * 5,
            *own, *halos,
        )
        field, face, layer = (
            (2, 2, LAYERS, EDGE, LANES),
            (2, 2, LAYERS, 2 * SUB, LANES),
            (2, 2, EDGE, LANES),
        )
        depth, soil = call(
            edges, shapes, [field] * 5 + [face] * 7 + [layer] * 5 + [(2, 4, NEAR, LANES)], *held, above, below
        )
        soil = lax.all_to_all(soil, "place", 0, 0)
        [soil] = call(
            scatter_blocks,
            [(LAYERS, 1, SUB, GROUP * LANES)],
            [pltpu.SemaphoreType.DMA((GROUP,))],
            soil,
            places=[pl.ANY, pltpu.HBM],
        )
        return depth, soil

    surface = P("sec", ("band", "place"))
    blocked = P(None, axes, None, None)
    return jax.shard_map(
        local,
        mesh=parts,
        in_specs=(surface, surface, surface, blocked, blocked),
        out_specs=(surface, blocked),
        check_vma=False,
    )
```

```python
import math

import jax
import jax.numpy as jnp
from jax import lax
from jax.experimental import pallas as pl
from jax.experimental.pallas import tpu as pltpu
from jax.sharding import Mesh
from jax.sharding import PartitionSpec as P

SWEEPS = 3
STEPS = 4
STORAGE = 0.3
ROUTING = 0.15
LEAKANCE = 0.25
SPECTRUM_MID = 1.025
SPECTRUM_HALF = 0.975

LAYERS = 5
GROUP = 8
HALO = SWEEPS * STEPS
SOIL = 2 * LAYERS
FIELDS = SOIL + 3
SUB = 8
LANES = 128
ROWS = 64
REACH = (HALO,) * SOIL + (HALO - 1, HALO - SWEEPS, HALO - SWEEPS - 1)
STARTS = tuple(sum(REACH[:field]) for field in range(FIELDS))
CORNERS = sum(REACH)
CORNERS_TOP = CORNERS + HALO
FOLD = 3 * HALO
STRIP = -(-(CORNERS_TOP + HALO // 3) // SUB) * SUB


def sweep_factors(number):
    return [
        1.0
        / (SPECTRUM_MID - SPECTRUM_HALF * math.cos(math.pi * (2 * k + 1) / (2 * number)))
        for k in range(number)
    ]


def lane_index(rows):
    return lax.broadcasted_iota(jnp.int32, (rows, LANES), 1)


def turn(value, shift):
    shift %= LANES
    return pltpu.roll(value, shift, 1) if shift else value


def own_rows(soil, surface, field, p):
    if field < SOIL:
        return soil[p, field]
    return surface[field - SOIL, pl.ds(p * SUB, SUB), :]


def pack_columns(soil, surface, left, right):
    lane = lane_index(SUB)
    for p in range(GROUP):
        for plane, fields in ((0, range(SOIL)), (1, range(SOIL, FIELDS))):
            lefts = jnp.zeros((SUB, LANES), jnp.float32)
            rights = jnp.zeros((SUB, LANES), jnp.float32)
            for slot, field in enumerate(fields):
                value = own_rows(soil, surface, field, p)
                here = (lane >= slot * HALO) & (lane < slot * HALO + HALO)
                lefts = jnp.where(here, turn(value, slot * HALO), lefts)
                rights = jnp.where(here, turn(value, slot * HALO + HALO), rights)
            left[plane, pl.ds(p * SUB, SUB), :] = lefts
            right[plane, pl.ds(p * SUB, SUB), :] = rights


def facing(edge):
    if edge == 0:
        return [(i, HALO - 2 - i, HALO - 1 - i) for i in range(HALO - 1)]
    return [(i, HALO - i, i) for i in range(1, HALO)]


def pack_rows(soil, surface, from_left, from_right, top, bottom, corner):
    lane = lane_index(1)
    column = lane
    for slot in range(1, LANES // HALO + 1):
        column = jnp.where(lane >= slot * HALO, lane - slot * HALO, column)
    for edge, out in enumerate((top, bottom)):
        for field in range(FIELDS):
            at, count = STARTS[field], REACH[field]
            rest = count - SUB
            if edge == 0:
                out[pl.ds(at, SUB), :] = own_rows(soil, surface, field, 0)
                if rest:
                    out[pl.ds(at + SUB, rest), :] = own_rows(soil, surface, field, 1)[:rest]
            else:
                if rest:
                    out[pl.ds(at, rest), :] = own_rows(soil, surface, field, GROUP - 2)[SUB - rest :]
                out[pl.ds(at + rest, SUB), :] = own_rows(soil, surface, field, GROUP - 1)
        first = edge * (ROWS - HALO)
        corner[...] = jnp.zeros((2 * SUB, LANES), jnp.float32)
        out[pl.ds(STRIP - SUB, SUB), :] = jnp.zeros((SUB, LANES), jnp.float32)
        for i, j, right in facing(edge):
            here, there = pl.ds(first + i, 1), pl.ds(first + j, 1)
            take = column < right
            out[pl.ds(CORNERS + i, 1), :] = jnp.where(
                take, from_right[0, here, :], from_left[0, there, :]
            )
            corner[pl.ds(i, 1), :] = jnp.where(
                take, from_right[1, here, :], from_left[1, there, :]
            )
        spare = 0 if edge else HALO - 1
        out[pl.ds(CORNERS + spare, 1), :] = jnp.zeros((1, LANES), jnp.float32)
        some = HALO // 3
        lanes = lane_index(some)
        out[pl.ds(CORNERS_TOP, some), :] = jnp.where(
            lanes < FOLD,
            corner[pl.ds(0, some), :],
            jnp.where(
                lanes < 2 * FOLD,
                turn(corner[pl.ds(some, some), :], FOLD),
                turn(corner[pl.ds(2 * some, some), :], 2 * FOLD),
            ),
        )


def beside(one, two, lane):
    r1, r2 = turn(one, -1), turn(two, -1)
    l1, l2 = turn(one, 1), turn(two, 1)
    last, first = lane == LANES - 1, lane == 0
    right = (jnp.where(last, r2, r1), jnp.where(last, r1, r2))
    left = (jnp.where(first, l2, l1), jnp.where(first, l1, l2))
    return right, left


def gather_blocks(
    pressure, conductance, depth, elevation, mask, pieces, surface, soil_here, mask_here, sems
):
    arriving = [
        pltpu.make_async_copy(source, goal, sems.at[i])
        for i, (source, goal) in enumerate(
            (
                (pressure.at[:, 0], soil_here.at[0]),
                (conductance.at[:, 0], soil_here.at[1]),
                (depth, surface.at[0]),
                (elevation, surface.at[1]),
                (mask, mask_here),
            )
        )
    ]
    for copy in arriving:
        copy.start()
    for half in range(2):
        arriving[half].wait()
        for j in range(GROUP):
            for layer in range(LAYERS):
                pieces[j, half * LAYERS + layer] = soil_here[
                    half, layer, :, pl.ds(j * LANES, LANES)
                ]
    for copy in arriving[2:]:
        copy.wait()
    surface[2] = mask_here[...].astype(jnp.float32)


def scatter_blocks(pieces, pressure, sems):
    copies = [
        pltpu.make_async_copy(
            pieces.at[j], pressure.at[:, 0, :, pl.ds(j * LANES, LANES)], sems.at[j]
        )
        for j in range(GROUP)
    ]
    for copy in copies:
        copy.start()
    for copy in copies:
        copy.wait()


def spread(lefts, rights, lane, slot):
    return jnp.where(
        lane < HALO,
        turn(rights, -slot * HALO),
        jnp.where(lane >= LANES - HALO, turn(lefts, LANES - HALO - slot * HALO), 0.0),
    )


PLANES = range(2)


class Field:
    def __init__(self, ref, *where):
        self.ref, self.where = ref, where

    def __getitem__(self, key):
        return self.ref[self.where + key]

    def __setitem__(self, key, value):
        self.ref[self.where + key] = value


def set_conduct(rows, K, U, C, D, E, H, B):
    for plane in PLANES:
        depth = D[plane, rows, :]
        H[plane, rows, :] = depth + E[plane, rows, :]
        B[plane, rows, :] = jnp.where(
            K[plane, 0, rows, :] > 0, 1.0 + 0.5 * jnp.tanh(depth), 0.0
        )
        for layer in range(LAYERS):
            u = U[plane, layer, rows, :]
            C[plane, layer, rows, :] = 0.5 * K[plane, layer, rows, :] / (1.0 + u * u)


def around(row, wide):
    return pl.ds(row, wide), pl.ds(row - 1, wide), pl.ds(row + 1, wide)


def first_sweep(row, wide, at, lane, factor, K, U, X, C, D, M, H, B, faces):
    east, west, south, north, down, inverse, side = faces
    rows, before, after = around(row, wide)
    head = [H[plane, rows, :] for plane in PLANES]
    mobile = [B[plane, rows, :] for plane in PLANES]
    head_sides = beside(*head, lane)
    mobile_sides = beside(*mobile, lane)
    flux = []
    for plane in PLANES:
        depth = D[plane, rows, :]
        now = LEAKANCE * (depth - U[plane, 0, rows, :])
        flux.append(now)
        change = jnp.zeros_like(depth)
        for other_head, other_mobile in (
            (H[plane, after, :], B[plane, after, :]),
            (H[plane, before, :], B[plane, before, :]),
            (head_sides[0][plane], mobile_sides[0][plane]),
            (head_sides[1][plane], mobile_sides[1][plane]),
        ):
            change = change + (mobile[plane] + other_mobile) * (other_head - head[plane])
        D[plane, rows, :] = M[plane, rows, :] * (depth + (0.5 * ROUTING) * change - now)
    conduct = [[C[plane, layer, rows, :] for layer in range(LAYERS)] for plane in PLANES]
    iterate = [[U[plane, layer, rows, :] for layer in range(LAYERS)] for plane in PLANES]
    between = [
        [2.0 * (conduct[plane][l] + conduct[plane][l + 1]) for l in range(LAYERS - 1)]
        for plane in PLANES
    ]
    for layer in range(LAYERS):
        c_right, c_left = beside(conduct[0][layer], conduct[1][layer], lane)
        u_right, u_left = beside(iterate[0][layer], iterate[1][layer], lane)
        for plane in PLANES:
            c, u = conduct[plane][layer], iterate[plane][layer]
            e, w = c + c_right[plane], c + c_left[plane]
            s, n = c + C[plane, layer, after, :], c + C[plane, layer, before, :]
            diagonal = (STORAGE + e) + w + (s + n)
            total = STORAGE * u
            if layer == 0:
                total = total + flux[plane]
            side[plane, layer, at, :] = total
            total = total + e * u_right[plane] + w * u_left[plane]
            total = total + s * U[plane, layer, after, :] + n * U[plane, layer, before, :]
            if layer > 0:
                diagonal = diagonal + between[plane][layer - 1]
                total = total + between[plane][layer - 1] * iterate[plane][layer - 1]
            if layer < LAYERS - 1:
                diagonal = diagonal + between[plane][layer]
                total = total + between[plane][layer] * iterate[plane][layer + 1]
                down[plane, layer, at, :] = between[plane][layer]
            inv = jnp.where(K[plane, layer, rows, :] > 0, 1.0 / diagonal, 0.0)
            east[plane, layer, at, :] = e
            west[plane, layer, at, :] = w
            south[plane, layer, at, :] = s
            north[plane, layer, at, :] = n
            inverse[plane, layer, at, :] = inv
            X[plane, layer, rows, :] = (1.0 - factor) * u + factor * (inv * total)


def later_sweep(row, wide, at, lane, factor, source, goal, faces):
    east, west, south, north, down, inverse, side = faces
    rows, before, after = around(row, wide)
    iterate = [[source[plane, layer, rows, :] for layer in range(LAYERS)] for plane in PLANES]
    between = [[down[plane, layer, at, :] for layer in range(LAYERS - 1)] for plane in PLANES]
    for layer in range(LAYERS):
        u_right, u_left = beside(iterate[0][layer], iterate[1][layer], lane)
        for plane in PLANES:
            u = iterate[plane][layer]
            total = side[plane, layer, at, :]
            total = total + east[plane, layer, at, :] * u_right[plane]
            total = total + west[plane, layer, at, :] * u_left[plane]
            total = total + south[plane, layer, at, :] * source[plane, layer, after, :]
            total = total + north[plane, layer, at, :] * source[plane, layer, before, :]
            if layer > 0:
                total = total + between[plane][layer - 1] * iterate[plane][layer - 1]
            if layer < LAYERS - 1:
                total = total + between[plane][layer] * iterate[plane][layer + 1]
            inv = inverse[plane, layer, at, :]
            goal[plane, layer, rows, :] = (1.0 - factor) * u + factor * (inv * total)


NEAR = 16
TOPS = (SUB, SUB + ROWS - NEAR)
INNER = SUB + ROWS + SUB


def clear(refs, rows):
    for ref in refs:
        lead = ref.shape[:-2]
        value = jnp.zeros((rows.size, LANES), jnp.float32)
        for flat in range(math.prod(lead)):
            where = []
            for size in reversed(lead):
                where.insert(0, flat % size)
                flat //= size
            ref[tuple(where) + (rows, slice(None))] = value


def inner(
    soil, surface, from_left, from_right,
    depth_out, pressure_out, seen, seen_k, seen_d, seen_e, seen_m,
    K, U, X, Y, C, east, west, south, north, down, inverse, side, D, E, M, H, B,
):
    factors = sweep_factors(SWEEPS)
    faces = (east, west, south, north, down, inverse, side)
    for row in (0, INNER - SUB):
        clear((K, U, X, Y, C, D, E, M, H, B), pl.ds(row, SUB))
    lane = lane_index(SUB)
    for field in range(FIELDS):
        if field < SOIL:
            at, slot, half = Field((U, K)[field // LAYERS]), field, 0
            name = lambda plane, rows: (plane, field % LAYERS, rows, slice(None))
        else:
            at, slot, half = Field((D, E, M)[field - SOIL]), field - SOIL, 1
            name = lambda plane, rows: (plane, rows, slice(None))
        for p in range(GROUP):
            rows, here = pl.ds(SUB + p * SUB, SUB), pl.ds(p * SUB, SUB)
            at[name(0, rows)] = own_rows(soil, surface, field, p)
            at[name(1, rows)] = spread(
                from_left[half, here, :], from_right[half, here, :], lane, slot
            )

    def note(source, number):
        for edge, top in enumerate(TOPS):
            for plane in PLANES:
                for layer in range(LAYERS):
                    seen[number, edge, plane, layer] = source[plane, layer, pl.ds(top, NEAR), :]

    def note_depth(number):
        for edge, top in enumerate(TOPS):
            for plane in PLANES:
                seen_d[number, edge, plane] = D[plane, pl.ds(top, NEAR), :]

    note(U, 0)
    note_depth(0)
    for edge, top in enumerate(TOPS):
        rows = pl.ds(top, NEAR)
        for plane in PLANES:
            seen_e[edge, plane] = E[plane, rows, :]
            seen_m[edge, plane] = M[plane, rows, :]
            for layer in range(LAYERS):
                seen_k[edge, plane, layer] = K[plane, layer, rows, :]

    wide = 2 * SUB
    lane2 = lane_index(wide)

    def step(number):
        last = number == STEPS - 1
        low, trips = (2 * SUB, 3) if last else (SUB, 4)

        def loop(count, begin, body):
            for i in range(count):
                body(begin + wide * i)

        loop(4, SUB, lambda row: set_conduct(pl.ds(row, wide), K, U, C, D, E, H, B))
        loop(
            trips, low,
            lambda row: first_sweep(
                row, wide, pl.ds(row, wide), lane2, factors[0], K, U, X, C, D, M, H, B, faces
            ),
        )
        note(X, 3 * number + 1)
        loop(
            trips, low,
            lambda row: later_sweep(row, wide, pl.ds(row, wide), lane2, factors[1], X, Y, faces),
        )
        note(Y, 3 * number + 2)
        loop(
            trips, low,
            lambda row: later_sweep(row, wide, pl.ds(row, wide), lane2, factors[2], Y, U, faces),
        )

        if not last:
            note(U, 3 * number + 3)
            note_depth(number + 1)

    for number in range(STEPS):
        step(number)
    depth_out[...] = D[0, pl.ds(SUB, ROWS), :]
    for p in range(GROUP):
        for layer in range(LAYERS):
            pressure_out[p, layer] = U[0, layer, pl.ds(SUB + p * SUB, SUB), :]


EDGE = 56


def edges(
    inner_depth, inner_pressure, seen, seen_k, seen_d, seen_e, seen_m, above, below,
    depth_out, pressure_out,
    K, U, X, Y, C, east, west, south, north, down, inverse, side, D, E, M, H, B, corner,
):
    factors = sweep_factors(SWEEPS)
    wide = 2 * SUB
    everything = (K, U, X, Y, D, E, M)
    clear(everything, pl.ds(0, NEAR))
    clear(everything, pl.ds(2 * NEAR, EDGE - 2 * NEAR))
    clear((X, Y), pl.ds(NEAR, NEAR))
    lane = lane_index(HALO)
    some = HALO // 3
    own = pl.ds(NEAR, NEAR)
    clear((corner,), pl.ds(0, NEAR))
    for edge, packed in enumerate((above, below)):
        for part in range(3):
            corner[edge, 1, pl.ds(part * some, some), :] = turn(
                packed[pl.ds(CORNERS_TOP, some), :], -part * FOLD
            )
        corner[edge, 0, pl.ds(0, HALO), :] = packed[pl.ds(CORNERS, HALO), :]
        for i, j, _ in facing(1 - edge):
            for half in range(2):
                corner[edge, 2 + half, pl.ds(j, 1), :] = corner[edge, half, pl.ds(i, 1), :]
        whole = pl.ds(0, HALO)
        rows = pl.ds(2 * NEAR if edge else NEAR - HALO, HALO)
        for field in range(FIELDS):
            count = REACH[field]
            filled = pl.ds(2 * NEAR if edge else NEAR - count, count)
            value = packed[pl.ds(STARTS[field], count), :]
            half, slot = (0, field) if field < SOIL else (1, field - SOIL)
            sides = spread(
                corner[edge, 2 + half, whole, :], corner[edge, half, whole, :], lane, slot
            )
            if field < SOIL:
                ref, layer = (U, K)[field // LAYERS], field % LAYERS
                ref[edge, 0, layer, filled, :] = value
                ref[edge, 1, layer, rows, :] = sides
            else:
                ref = (D, E, M)[field - SOIL]
                ref[edge, 0, filled, :] = value
                ref[edge, 1, rows, :] = sides
        for plane in PLANES:
            D[edge, plane, own, :] = seen_d[0, edge, plane]
            E[edge, plane, own, :] = seen_e[edge, plane]
            M[edge, plane, own, :] = seen_m[edge, plane]
            for layer in range(LAYERS):
                U[edge, plane, layer, own, :] = seen[0, edge, plane, layer]
                K[edge, plane, layer, own, :] = seen_k[edge, plane, layer]

    lane2, lane3 = lane_index(wide), lane_index(3 * SUB)
    at = pl.ds(0, wide)

    def step(number):
        starts = (NEAR - 11 + 3 * number, 2 * NEAR - 5 - 3 * number)
        both = range(2)
        of = lambda ref: [Field(ref, edge) for edge in both]
        k, u, x, y, c, d, m, h, b = map(of, (K, U, X, Y, C, D, M, H, B))
        e = of(E)
        faces = [
            [Field(ref, edge) for ref in (east, west, south, north, down, inverse, side)]
            for edge in both
        ]

        def fill(goal, sweep, count):
            for edge in both:
                row = starts[0] + wide if edge == 0 else starts[1] - count
                for plane in PLANES:
                    for layer in range(LAYERS):
                        goal[edge, plane, layer, pl.ds(row, count), :] = seen[
                            sweep, edge, plane, layer, pl.ds(row - NEAR, count), :
                        ]

        for edge in both:
            rows = pl.ds(starts[edge] - 1, 3 * SUB)
            set_conduct(rows, k[edge], u[edge], c[edge], d[edge], e[edge], h[edge], b[edge])
        for edge in both:
            first_sweep(
                starts[edge], wide, at, lane2, factors[0],
                k[edge], u[edge], x[edge], c[edge], d[edge], m[edge], h[edge], b[edge], faces[edge],
            )
        fill(X, 3 * number + 1, 1)
        for edge in both:
            later_sweep(starts[edge], wide, at, lane2, factors[1], x[edge], y[edge], faces[edge])
        fill(Y, 3 * number + 2, 1)
        for edge in both:
            later_sweep(starts[edge], wide, at, lane2, factors[2], y[edge], u[edge], faces[edge])

        if number < STEPS - 1:
            fill(U, 3 * number + 3, 4)
            for edge in both:
                row = starts[0] + wide if edge == 0 else starts[1] - 4
                for plane in PLANES:
                    D[edge, plane, pl.ds(row, 4), :] = seen_d[
                        number + 1, edge, plane, pl.ds(row - NEAR, 4), :
                    ]

    for number in range(STEPS):
        step(number)
    left = ROWS - HALO
    depth_out[pl.ds(HALO, ROWS - 2 * HALO), :] = inner_depth[pl.ds(HALO, ROWS - 2 * HALO), :]
    depth_out[pl.ds(0, HALO), :] = D[0, 0, pl.ds(NEAR, HALO), :]
    depth_out[pl.ds(left, HALO), :] = D[1, 0, pl.ds(2 * NEAR - HALO, HALO), :]
    half = HALO - SUB
    for layer in range(LAYERS):
        for p in range(2, GROUP - 2):
            pressure_out[p, layer] = inner_pressure[p, layer]
        pressure_out[0, layer] = U[0, 0, layer, pl.ds(NEAR, SUB), :]
        pressure_out[1, layer, pl.ds(0, half), :] = U[0, 0, layer, pl.ds(NEAR + SUB, half), :]
        pressure_out[1, layer, pl.ds(half, SUB - half), :] = inner_pressure[
            1, layer, pl.ds(half, SUB - half), :
        ]
        pressure_out[GROUP - 2, layer, pl.ds(0, SUB - half), :] = inner_pressure[
            GROUP - 2, layer, pl.ds(0, SUB - half), :
        ]
        pressure_out[GROUP - 2, layer, pl.ds(SUB - half, half), :] = U[
            1, 0, layer, pl.ds(2 * NEAR - HALO, half), :
        ]
        pressure_out[GROUP - 1, layer] = U[1, 0, layer, pl.ds(2 * NEAR - SUB, SUB), :]


def call(kernel, outs, scratch, *args, places=None):
    places = places or [pltpu.VMEM] * (len(args) + len(outs))
    specs = [pl.BlockSpec(memory_space=place) for place in places]
    args = [
        pltpu.with_memory_space_constraint(arg, place) if place == pltpu.HBM else arg
        for arg, place in zip(args, places)
    ]
    return pl.pallas_call(
        kernel,
        out_shape=[jax.ShapeDtypeStruct(shape, jnp.float32) for shape in outs],
        in_specs=specs[: len(args)],
        out_specs=specs[len(args) :],
        scratch_shapes=[
            pltpu.VMEM(shape, jnp.float32) if isinstance(shape, tuple) else shape
            for shape in scratch
        ],
        compiler_params=pltpu.CompilerParams(vmem_limit_bytes=32 << 20),
    )(*args)


def solution(mesh):
    secs, tiles = mesh.shape["sec"], mesh.shape["tile"]
    axes = ("sec", "band", "place")
    parts = Mesh(mesh.devices.reshape(secs, tiles // GROUP, GROUP), axes)

    def pairs(along, odd):
        found = []
        for s in range(secs):
            for t in range(tiles):
                index, count = (s, secs) if along == "sec" else (t, tiles)
                other = index + 1 if index % 2 == odd else index - 1
                if 0 <= other < count:
                    goal = (other, t) if along == "sec" else (s, other)
                    found.append((s * tiles + t, goal[0] * tiles + goal[1]))
        return found

    def swap(value, along, odd):
        return lax.ppermute(value, axes, pairs(along, odd))

    def local(depth, elevation, land_mask, pressure, conductance):
        tile_odd = lax.axis_index("place") % 2 == 1
        sec_odd = lax.axis_index("sec") % 2 == 1
        pieces, surface = call(
            gather_blocks,
            [(GROUP, SOIL, SUB, LANES), (3, ROWS, LANES)],
            [
                (2, LAYERS, SUB, GROUP * LANES),
                pltpu.VMEM((ROWS, LANES), jnp.int32),
                pltpu.SemaphoreType.DMA((5,)),
            ],
            pressure, conductance, depth, elevation, land_mask,
            places=[pltpu.HBM] * 5 + [pltpu.VMEM] * 2,
        )
        pieces, tile_odd, sec_odd = lax.optimization_barrier((pieces, tile_odd, sec_odd))
        soil = lax.all_to_all(pieces, "place", 0, 0)
        own = (soil, surface)
        left, right = call(pack_columns, [(2, ROWS, LANES)] * 2, [], *own)
        one = swap(jnp.where(tile_odd, left, right), "tile", 0)
        two = swap(jnp.where(tile_odd, right, left), "tile", 1)
        from_left = jnp.where(tile_odd, one, two)
        from_right = jnp.where(tile_odd, two, one)
        top, bottom = call(
            pack_rows, [(STRIP, LANES)] * 2, [(2 * SUB, LANES)], *own, from_left, from_right
        )
        one = swap(jnp.where(sec_odd, bottom, top), "sec", 1)
        two = swap(jnp.where(sec_odd, top, bottom), "sec", 0)
        above = jnp.where(sec_odd, two, one)
        below = jnp.where(sec_odd, one, two)
        near = (2, 2, LAYERS, NEAR, LANES)
        field, layer = (2, LAYERS, INNER, LANES), (2, INNER, LANES)
        shapes = [(ROWS, LANES), (GROUP, LAYERS, SUB, LANES)]
        held = call(
            inner,
            shapes + [(SWEEPS * STEPS,) + near, near, (STEPS, 2, 2, NEAR, LANES)] + [(2, 2, NEAR, LANES)] * 2,
            [field] * 12 + [layer] * 5,
            *own, from_left, from_right,
        )
        field, face, layer = (
            (2, 2, LAYERS, EDGE, LANES),
            (2, 2, LAYERS, 2 * SUB, LANES),
            (2, 2, EDGE, LANES),
        )
        depth, soil = call(
            edges, shapes, [field] * 5 + [face] * 7 + [layer] * 5 + [(2, 4, NEAR, LANES)], *held, above, below
        )
        soil = lax.all_to_all(soil, "place", 0, 0)
        [soil] = call(
            scatter_blocks,
            [(LAYERS, 1, SUB, GROUP * LANES)],
            [pltpu.SemaphoreType.DMA((GROUP,))],
            soil,
            places=[pl.ANY, pltpu.HBM],
        )
        return depth, soil

    surface = P("sec", ("band", "place"))
    blocked = P(None, axes, None, None)
    return jax.shard_map(
        local,
        mesh=parts,
        in_specs=(surface, surface, surface, blocked, blocked),
        out_specs=(surface, blocked),
        check_vma=False,
    )
```

```python
import math

import jax
import jax.numpy as jnp
from jax import lax
from jax.experimental import pallas as pl
from jax.experimental.pallas import tpu as pltpu
from jax.sharding import Mesh
from jax.sharding import PartitionSpec as P

SWEEPS = 3
STEPS = 4
STORAGE = 0.3
ROUTING = 0.15
LEAKANCE = 0.25
SPECTRUM_MID = 1.025
SPECTRUM_HALF = 0.975

LAYERS = 5
GROUP = 8
HALO = SWEEPS * STEPS
SOIL = 2 * LAYERS
FIELDS = SOIL + 3
SUB = 8
LANES = 128
ROWS = 64
REACH = (HALO,) * SOIL + (HALO - 1, HALO - SWEEPS, HALO - SWEEPS - 1)
STARTS = tuple(sum(REACH[:field]) for field in range(FIELDS))
CORNERS = sum(REACH)
CORNERS_TOP = CORNERS + HALO
FOLD = 3 * HALO
STRIP = -(-(CORNERS_TOP + HALO // 3) // SUB) * SUB


def sweep_factors(number):
    return [
        1.0
        / (SPECTRUM_MID - SPECTRUM_HALF * math.cos(math.pi * (2 * k + 1) / (2 * number)))
        for k in range(number)
    ]


def lane_index(rows):
    return lax.broadcasted_iota(jnp.int32, (rows, LANES), 1)


def turn(value, shift):
    shift %= LANES
    return pltpu.roll(value, shift, 1) if shift else value


def own_rows(soil, surface, field, p):
    if field < SOIL:
        return soil[p, field]
    return surface[field - SOIL, pl.ds(p * SUB, SUB), :]


FOLDED = 3 * SUB
TALL = ROWS + FOLDED


def pack_columns(soil, surface, left, right):
    lane = lane_index(SUB)
    folded = [[jnp.zeros((SUB, LANES), jnp.float32)] * 3 for _ in range(2)]
    for p in range(GROUP):
        for plane, fields in ((0, range(SOIL)), (1, range(SOIL, FIELDS))):
            ends = [jnp.zeros((SUB, LANES), jnp.float32)] * 2
            for slot, field in enumerate(fields):
                value = own_rows(soil, surface, field, p)
                here = (lane >= slot * HALO) & (lane < slot * HALO + HALO)
                ends = [
                    jnp.where(here, turn(value, slot * HALO + HALO * end), ends[end])
                    for end in range(2)
                ]
            for end, out in enumerate((left, right)):
                if plane == 0:
                    out[pl.ds(p * SUB, SUB), :] = ends[end]
                else:
                    folded[end][p % 3] += turn(ends[end], FOLD * (p // 3))
    for end, out in enumerate((left, right)):
        for part in range(3):
            out[pl.ds(ROWS + part * SUB, SUB), :] = folded[end][part]


def unfolded(packed, row, count):
    group, first = divmod(row, FOLDED)
    return turn(packed[pl.ds(ROWS + first, count), :], -FOLD * group)


def facing(edge):
    if edge == 0:
        return [(i, HALO - 2 - i, HALO - 1 - i) for i in range(HALO - 1)]
    return [(i, HALO - i, i) for i in range(1, HALO)]


def pack_rows(soil, surface, from_left, from_right, top, bottom, corner):
    lane = lane_index(1)
    column = lane
    for slot in range(1, LANES // HALO + 1):
        column = jnp.where(lane >= slot * HALO, lane - slot * HALO, column)
    for edge, out in enumerate((top, bottom)):
        for field in range(FIELDS):
            at, count = STARTS[field], REACH[field]
            rest = count - SUB
            if edge == 0:
                out[pl.ds(at, SUB), :] = own_rows(soil, surface, field, 0)
                if rest:
                    out[pl.ds(at + SUB, rest), :] = own_rows(soil, surface, field, 1)[:rest]
            else:
                if rest:
                    out[pl.ds(at, rest), :] = own_rows(soil, surface, field, GROUP - 2)[SUB - rest :]
                out[pl.ds(at + rest, SUB), :] = own_rows(soil, surface, field, GROUP - 1)
        first = edge * (ROWS - HALO)
        corner[...] = jnp.zeros((2 * SUB, LANES), jnp.float32)
        out[pl.ds(STRIP - SUB, SUB), :] = jnp.zeros((SUB, LANES), jnp.float32)
        for i, j, right in facing(edge):
            take = column < right
            out[pl.ds(CORNERS + i, 1), :] = jnp.where(
                take, from_right[pl.ds(first + i, 1), :], from_left[pl.ds(first + j, 1), :]
            )
            corner[pl.ds(i, 1), :] = jnp.where(
                take, unfolded(from_right, first + i, 1), unfolded(from_left, first + j, 1)
            )
        spare = 0 if edge else HALO - 1
        out[pl.ds(CORNERS + spare, 1), :] = jnp.zeros((1, LANES), jnp.float32)
        some = HALO // 3
        lanes = lane_index(some)
        out[pl.ds(CORNERS_TOP, some), :] = jnp.where(
            lanes < FOLD,
            corner[pl.ds(0, some), :],
            jnp.where(
                lanes < 2 * FOLD,
                turn(corner[pl.ds(some, some), :], FOLD),
                turn(corner[pl.ds(2 * some, some), :], 2 * FOLD),
            ),
        )


def beside(one, two, lane):
    r1, r2 = turn(one, -1), turn(two, -1)
    l1, l2 = turn(one, 1), turn(two, 1)
    last, first = lane == LANES - 1, lane == 0
    right = (jnp.where(last, r2, r1), jnp.where(last, r1, r2))
    left = (jnp.where(first, l2, l1), jnp.where(first, l1, l2))
    return right, left


def gather_blocks(
    pressure, conductance, depth, elevation, mask, pieces, surface, soil_here, mask_here, sems
):
    arriving = [
        pltpu.make_async_copy(source, goal, sems.at[i])
        for i, (source, goal) in enumerate(
            (
                (pressure.at[:, 0], soil_here.at[0]),
                (conductance.at[:, 0], soil_here.at[1]),
                (depth, surface.at[0]),
                (elevation, surface.at[1]),
                (mask, mask_here),
            )
        )
    ]
    for copy in arriving:
        copy.start()
    for half in range(2):
        arriving[half].wait()
        for j in range(GROUP):
            for layer in range(LAYERS):
                pieces[j, half * LAYERS + layer] = soil_here[
                    half, layer, :, pl.ds(j * LANES, LANES)
                ]
    for copy in arriving[2:]:
        copy.wait()
    surface[2] = mask_here[...].astype(jnp.float32)


def scatter_blocks(pieces, pressure, sems):
    copies = [
        pltpu.make_async_copy(
            pieces.at[j], pressure.at[:, 0, :, pl.ds(j * LANES, LANES)], sems.at[j]
        )
        for j in range(GROUP)
    ]
    for copy in copies:
        copy.start()
    for copy in copies:
        copy.wait()


def spread(lefts, rights, lane, slot):
    return jnp.where(
        lane < HALO,
        turn(rights, -slot * HALO),
        jnp.where(lane >= LANES - HALO, turn(lefts, LANES - HALO - slot * HALO), 0.0),
    )


PLANES = range(2)


class Field:
    def __init__(self, ref, *where):
        self.ref, self.where = ref, where

    def __getitem__(self, key):
        return self.ref[self.where + key]

    def __setitem__(self, key, value):
        self.ref[self.where + key] = value


def set_conduct(rows, K, U, C, D, E, H, B):
    for plane in PLANES:
        depth = D[plane, rows, :]
        H[plane, rows, :] = depth + E[plane, rows, :]
        B[plane, rows, :] = jnp.where(
            K[plane, 0, rows, :] > 0, 1.0 + 0.5 * jnp.tanh(depth), 0.0
        )
        for layer in range(LAYERS):
            u = U[plane, layer, rows, :]
            C[plane, layer, rows, :] = 0.5 * K[plane, layer, rows, :] / (1.0 + u * u)


def around(row, wide):
    return pl.ds(row, wide), pl.ds(row - 1, wide), pl.ds(row + 1, wide)


def first_sweep(row, wide, at, lane, factor, K, U, X, C, D, M, H, B, faces):
    east, west, south, north, down, inverse, side = faces
    rows, before, after = around(row, wide)
    head = [H[plane, rows, :] for plane in PLANES]
    mobile = [B[plane, rows, :] for plane in PLANES]
    head_sides = beside(*head, lane)
    mobile_sides = beside(*mobile, lane)
    flux = []
    for plane in PLANES:
        depth = D[plane, rows, :]
        now = LEAKANCE * (depth - U[plane, 0, rows, :])
        flux.append(now)
        change = jnp.zeros_like(depth)
        for other_head, other_mobile in (
            (H[plane, after, :], B[plane, after, :]),
            (H[plane, before, :], B[plane, before, :]),
            (head_sides[0][plane], mobile_sides[0][plane]),
            (head_sides[1][plane], mobile_sides[1][plane]),
        ):
            change = change + (mobile[plane] + other_mobile) * (other_head - head[plane])
        D[plane, rows, :] = M[plane, rows, :] * (depth + (0.5 * ROUTING) * change - now)
    conduct = [[C[plane, layer, rows, :] for layer in range(LAYERS)] for plane in PLANES]
    iterate = [[U[plane, layer, rows, :] for layer in range(LAYERS)] for plane in PLANES]
    between = [
        [2.0 * (conduct[plane][l] + conduct[plane][l + 1]) for l in range(LAYERS - 1)]
        for plane in PLANES
    ]
    for layer in range(LAYERS):
        c_right, c_left = beside(conduct[0][layer], conduct[1][layer], lane)
        u_right, u_left = beside(iterate[0][layer], iterate[1][layer], lane)
        for plane in PLANES:
            c, u = conduct[plane][layer], iterate[plane][layer]
            e, w = c + c_right[plane], c + c_left[plane]
            s, n = c + C[plane, layer, after, :], c + C[plane, layer, before, :]
            diagonal = (STORAGE + e) + w + (s + n)
            total = STORAGE * u
            if layer == 0:
                total = total + flux[plane]
            side[plane, layer, at, :] = total
            total = total + e * u_right[plane] + w * u_left[plane]
            total = total + s * U[plane, layer, after, :] + n * U[plane, layer, before, :]
            if layer > 0:
                diagonal = diagonal + between[plane][layer - 1]
                total = total + between[plane][layer - 1] * iterate[plane][layer - 1]
            if layer < LAYERS - 1:
                diagonal = diagonal + between[plane][layer]
                total = total + between[plane][layer] * iterate[plane][layer + 1]
                down[plane, layer, at, :] = between[plane][layer]
            inv = jnp.where(K[plane, layer, rows, :] > 0, 1.0 / diagonal, 0.0)
            east[plane, layer, at, :] = e
            west[plane, layer, at, :] = w
            south[plane, layer, at, :] = s
            north[plane, layer, at, :] = n
            inverse[plane, layer, at, :] = inv
            X[plane, layer, rows, :] = (1.0 - factor) * u + factor * (inv * total)


def later_sweep(row, wide, at, lane, factor, source, goal, faces):
    east, west, south, north, down, inverse, side = faces
    rows, before, after = around(row, wide)
    iterate = [[source[plane, layer, rows, :] for layer in range(LAYERS)] for plane in PLANES]
    between = [[down[plane, layer, at, :] for layer in range(LAYERS - 1)] for plane in PLANES]
    for layer in range(LAYERS):
        u_right, u_left = beside(iterate[0][layer], iterate[1][layer], lane)
        for plane in PLANES:
            u = iterate[plane][layer]
            total = side[plane, layer, at, :]
            total = total + east[plane, layer, at, :] * u_right[plane]
            total = total + west[plane, layer, at, :] * u_left[plane]
            total = total + south[plane, layer, at, :] * source[plane, layer, after, :]
            total = total + north[plane, layer, at, :] * source[plane, layer, before, :]
            if layer > 0:
                total = total + between[plane][layer - 1] * iterate[plane][layer - 1]
            if layer < LAYERS - 1:
                total = total + between[plane][layer] * iterate[plane][layer + 1]
            inv = inverse[plane, layer, at, :]
            goal[plane, layer, rows, :] = (1.0 - factor) * u + factor * (inv * total)


NEAR = 16
TOPS = (SUB, SUB + ROWS - NEAR)
INNER = SUB + ROWS + SUB


def clear(refs, rows):
    for ref in refs:
        lead = ref.shape[:-2]
        value = jnp.zeros((rows.size, LANES), jnp.float32)
        for flat in range(math.prod(lead)):
            where = []
            for size in reversed(lead):
                where.insert(0, flat % size)
                flat //= size
            ref[tuple(where) + (rows, slice(None))] = value


def inner(
    soil, surface, from_left, from_right,
    depth_out, pressure_out, seen, seen_k, seen_d, seen_e, seen_m,
    K, U, X, Y, C, east, west, south, north, down, inverse, side, D, E, M, H, B,
):
    factors = sweep_factors(SWEEPS)
    faces = (east, west, south, north, down, inverse, side)
    for row in (0, INNER - SUB):
        clear((K, U, X, Y, C, D, E, M, H, B), pl.ds(row, SUB))
    lane = lane_index(SUB)
    for field in range(FIELDS):
        if field < SOIL:
            at, slot, half = Field((U, K)[field // LAYERS]), field, 0
            name = lambda plane, rows: (plane, field % LAYERS, rows, slice(None))
        else:
            at, slot, half = Field((D, E, M)[field - SOIL]), field - SOIL, 1
            name = lambda plane, rows: (plane, rows, slice(None))
        for p in range(GROUP):
            rows = pl.ds(SUB + p * SUB, SUB)
            at[name(0, rows)] = own_rows(soil, surface, field, p)
            sides = [
                unfolded(packed, p * SUB, SUB) if half else packed[pl.ds(p * SUB, SUB), :]
                for packed in (from_left, from_right)
            ]
            at[name(1, rows)] = spread(*sides, lane, slot)

    def note(source, number):
        for edge, top in enumerate(TOPS):
            for plane in PLANES:
                for layer in range(LAYERS):
                    seen[number, edge, plane, layer] = source[plane, layer, pl.ds(top, NEAR), :]

    def note_depth(number):
        for edge, top in enumerate(TOPS):
            for plane in PLANES:
                seen_d[number, edge, plane] = D[plane, pl.ds(top, NEAR), :]

    note(U, 0)
    note_depth(0)
    for edge, top in enumerate(TOPS):
        rows = pl.ds(top, NEAR)
        for plane in PLANES:
            seen_e[edge, plane] = E[plane, rows, :]
            seen_m[edge, plane] = M[plane, rows, :]
            for layer in range(LAYERS):
                seen_k[edge, plane, layer] = K[plane, layer, rows, :]

    wide = 2 * SUB
    lane2 = lane_index(wide)

    def step(number):
        last = number == STEPS - 1
        low, trips = (2 * SUB, 3) if last else (SUB, 4)

        def loop(count, begin, body):
            for i in range(count):
                body(begin + wide * i)

        loop(4, SUB, lambda row: set_conduct(pl.ds(row, wide), K, U, C, D, E, H, B))
        loop(
            trips, low,
            lambda row: first_sweep(
                row, wide, pl.ds(row, wide), lane2, factors[0], K, U, X, C, D, M, H, B, faces
            ),
        )
        note(X, 3 * number + 1)
        loop(
            trips, low,
            lambda row: later_sweep(row, wide, pl.ds(row, wide), lane2, factors[1], X, Y, faces),
        )
        note(Y, 3 * number + 2)
        loop(
            trips, low,
            lambda row: later_sweep(row, wide, pl.ds(row, wide), lane2, factors[2], Y, U, faces),
        )

        if not last:
            note(U, 3 * number + 3)
            note_depth(number + 1)

    for number in range(STEPS):
        step(number)
    depth_out[...] = D[0, pl.ds(SUB, ROWS), :]
    for p in range(GROUP):
        for layer in range(LAYERS):
            pressure_out[p, layer] = U[0, layer, pl.ds(SUB + p * SUB, SUB), :]


EDGE = 56


def edges(
    inner_depth, inner_pressure, seen, seen_k, seen_d, seen_e, seen_m, above, below,
    depth_out, pressure_out,
    K, U, X, Y, C, east, west, south, north, down, inverse, side, D, E, M, H, B, corner,
):
    factors = sweep_factors(SWEEPS)
    wide = 2 * SUB
    everything = (K, U, X, Y, D, E, M)
    clear(everything, pl.ds(0, NEAR))
    clear(everything, pl.ds(2 * NEAR, EDGE - 2 * NEAR))
    clear((X, Y), pl.ds(NEAR, NEAR))
    lane = lane_index(HALO)
    some = HALO // 3
    own = pl.ds(NEAR, NEAR)
    clear((corner,), pl.ds(0, NEAR))
    for edge, packed in enumerate((above, below)):
        for part in range(3):
            corner[edge, 1, pl.ds(part * some, some), :] = turn(
                packed[pl.ds(CORNERS_TOP, some), :], -part * FOLD
            )
        corner[edge, 0, pl.ds(0, HALO), :] = packed[pl.ds(CORNERS, HALO), :]
        for i, j, _ in facing(1 - edge):
            for half in range(2):
                corner[edge, 2 + half, pl.ds(j, 1), :] = corner[edge, half, pl.ds(i, 1), :]
        whole = pl.ds(0, HALO)
        rows = pl.ds(2 * NEAR if edge else NEAR - HALO, HALO)
        for field in range(FIELDS):
            count = REACH[field]
            filled = pl.ds(2 * NEAR if edge else NEAR - count, count)
            value = packed[pl.ds(STARTS[field], count), :]
            half, slot = (0, field) if field < SOIL else (1, field - SOIL)
            sides = spread(
                corner[edge, 2 + half, whole, :], corner[edge, half, whole, :], lane, slot
            )
            if field < SOIL:
                ref, layer = (U, K)[field // LAYERS], field % LAYERS
                ref[edge, 0, layer, filled, :] = value
                ref[edge, 1, layer, rows, :] = sides
            else:
                ref = (D, E, M)[field - SOIL]
                ref[edge, 0, filled, :] = value
                ref[edge, 1, rows, :] = sides
        for plane in PLANES:
            D[edge, plane, own, :] = seen_d[0, edge, plane]
            E[edge, plane, own, :] = seen_e[edge, plane]
            M[edge, plane, own, :] = seen_m[edge, plane]
            for layer in range(LAYERS):
                U[edge, plane, layer, own, :] = seen[0, edge, plane, layer]
                K[edge, plane, layer, own, :] = seen_k[edge, plane, layer]

    lane2, lane3 = lane_index(wide), lane_index(3 * SUB)
    at = pl.ds(0, wide)

    def step(number):
        starts = (NEAR - 11 + 3 * number, 2 * NEAR - 5 - 3 * number)
        both = range(2)
        of = lambda ref: [Field(ref, edge) for edge in both]
        k, u, x, y, c, d, m, h, b = map(of, (K, U, X, Y, C, D, M, H, B))
        e = of(E)
        faces = [
            [Field(ref, edge) for ref in (east, west, south, north, down, inverse, side)]
            for edge in both
        ]

        def fill(goal, sweep, count):
            for edge in both:
                row = starts[0] + wide if edge == 0 else starts[1] - count
                for plane in PLANES:
                    for layer in range(LAYERS):
                        goal[edge, plane, layer, pl.ds(row, count), :] = seen[
                            sweep, edge, plane, layer, pl.ds(row - NEAR, count), :
                        ]

        for edge in both:
            rows = pl.ds(starts[edge] - 1, 3 * SUB)
            set_conduct(rows, k[edge], u[edge], c[edge], d[edge], e[edge], h[edge], b[edge])
        for edge in both:
            first_sweep(
                starts[edge], wide, at, lane2, factors[0],
                k[edge], u[edge], x[edge], c[edge], d[edge], m[edge], h[edge], b[edge], faces[edge],
            )
        fill(X, 3 * number + 1, 1)
        for edge in both:
            later_sweep(starts[edge], wide, at, lane2, factors[1], x[edge], y[edge], faces[edge])
        fill(Y, 3 * number + 2, 1)
        for edge in both:
            later_sweep(starts[edge], wide, at, lane2, factors[2], y[edge], u[edge], faces[edge])

        if number < STEPS - 1:
            fill(U, 3 * number + 3, 4)
            for edge in both:
                row = starts[0] + wide if edge == 0 else starts[1] - 4
                for plane in PLANES:
                    D[edge, plane, pl.ds(row, 4), :] = seen_d[
                        number + 1, edge, plane, pl.ds(row - NEAR, 4), :
                    ]

    for number in range(STEPS):
        step(number)
    left = ROWS - HALO
    depth_out[pl.ds(HALO, ROWS - 2 * HALO), :] = inner_depth[pl.ds(HALO, ROWS - 2 * HALO), :]
    depth_out[pl.ds(0, HALO), :] = D[0, 0, pl.ds(NEAR, HALO), :]
    depth_out[pl.ds(left, HALO), :] = D[1, 0, pl.ds(2 * NEAR - HALO, HALO), :]
    half = HALO - SUB
    for layer in range(LAYERS):
        for p in range(2, GROUP - 2):
            pressure_out[p, layer] = inner_pressure[p, layer]
        pressure_out[0, layer] = U[0, 0, layer, pl.ds(NEAR, SUB), :]
        pressure_out[1, layer, pl.ds(0, half), :] = U[0, 0, layer, pl.ds(NEAR + SUB, half), :]
        pressure_out[1, layer, pl.ds(half, SUB - half), :] = inner_pressure[
            1, layer, pl.ds(half, SUB - half), :
        ]
        pressure_out[GROUP - 2, layer, pl.ds(0, SUB - half), :] = inner_pressure[
            GROUP - 2, layer, pl.ds(0, SUB - half), :
        ]
        pressure_out[GROUP - 2, layer, pl.ds(SUB - half, half), :] = U[
            1, 0, layer, pl.ds(2 * NEAR - HALO, half), :
        ]
        pressure_out[GROUP - 1, layer] = U[1, 0, layer, pl.ds(2 * NEAR - SUB, SUB), :]


def call(kernel, outs, scratch, *args, places=None):
    places = places or [pltpu.VMEM] * (len(args) + len(outs))
    specs = [pl.BlockSpec(memory_space=place) for place in places]
    args = [
        pltpu.with_memory_space_constraint(arg, place) if place == pltpu.HBM else arg
        for arg, place in zip(args, places)
    ]
    return pl.pallas_call(
        kernel,
        out_shape=[jax.ShapeDtypeStruct(shape, jnp.float32) for shape in outs],
        in_specs=specs[: len(args)],
        out_specs=specs[len(args) :],
        scratch_shapes=[
            pltpu.VMEM(shape, jnp.float32) if isinstance(shape, tuple) else shape
            for shape in scratch
        ],
        compiler_params=pltpu.CompilerParams(vmem_limit_bytes=32 << 20),
    )(*args)


def solution(mesh):
    secs, tiles = mesh.shape["sec"], mesh.shape["tile"]
    axes = ("sec", "band", "place")
    parts = Mesh(mesh.devices.reshape(secs, tiles // GROUP, GROUP), axes)

    def pairs(along, odd):
        found = []
        for s in range(secs):
            for t in range(tiles):
                index, count = (s, secs) if along == "sec" else (t, tiles)
                other = index + 1 if index % 2 == odd else index - 1
                if 0 <= other < count:
                    goal = (other, t) if along == "sec" else (s, other)
                    found.append((s * tiles + t, goal[0] * tiles + goal[1]))
        return found

    def swap(value, along, odd):
        return lax.ppermute(value, axes, pairs(along, odd))

    def local(depth, elevation, land_mask, pressure, conductance):
        tile_odd = lax.axis_index("place") % 2 == 1
        sec_odd = lax.axis_index("sec") % 2 == 1
        pieces, surface = call(
            gather_blocks,
            [(GROUP, SOIL, SUB, LANES), (3, ROWS, LANES)],
            [
                (2, LAYERS, SUB, GROUP * LANES),
                pltpu.VMEM((ROWS, LANES), jnp.int32),
                pltpu.SemaphoreType.DMA((5,)),
            ],
            pressure, conductance, depth, elevation, land_mask,
            places=[pltpu.HBM] * 5 + [pltpu.VMEM] * 2,
        )
        pieces, tile_odd, sec_odd = lax.optimization_barrier((pieces, tile_odd, sec_odd))
        soil = lax.all_to_all(pieces, "place", 0, 0)
        own = (soil, surface)
        left, right = call(pack_columns, [(TALL, LANES)] * 2, [], *own)
        one = swap(jnp.where(tile_odd, left, right), "tile", 0)
        two = swap(jnp.where(tile_odd, right, left), "tile", 1)
        from_left = jnp.where(tile_odd, one, two)
        from_right = jnp.where(tile_odd, two, one)
        top, bottom = call(
            pack_rows, [(STRIP, LANES)] * 2, [(2 * SUB, LANES)], *own, from_left, from_right
        )
        one = swap(jnp.where(sec_odd, bottom, top), "sec", 1)
        two = swap(jnp.where(sec_odd, top, bottom), "sec", 0)
        above = jnp.where(sec_odd, two, one)
        below = jnp.where(sec_odd, one, two)
        near = (2, 2, LAYERS, NEAR, LANES)
        field, layer = (2, LAYERS, INNER, LANES), (2, INNER, LANES)
        shapes = [(ROWS, LANES), (GROUP, LAYERS, SUB, LANES)]
        held = call(
            inner,
            shapes + [(SWEEPS * STEPS,) + near, near, (STEPS, 2, 2, NEAR, LANES)] + [(2, 2, NEAR, LANES)] * 2,
            [field] * 12 + [layer] * 5,
            *own, from_left, from_right,
        )
        field, face, layer = (
            (2, 2, LAYERS, EDGE, LANES),
            (2, 2, LAYERS, 2 * SUB, LANES),
            (2, 2, EDGE, LANES),
        )
        depth, soil = call(
            edges, shapes, [field] * 5 + [face] * 7 + [layer] * 5 + [(2, 4, NEAR, LANES)], *held, above, below
        )
        soil = lax.all_to_all(soil, "place", 0, 0)
        [soil] = call(
            scatter_blocks,
            [(LAYERS, 1, SUB, GROUP * LANES)],
            [pltpu.SemaphoreType.DMA((GROUP,))],
            soil,
            places=[pl.ANY, pltpu.HBM],
        )
        return depth, soil

    surface = P("sec", ("band", "place"))
    blocked = P(None, axes, None, None)
    return jax.shard_map(
        local,
        mesh=parts,
        in_specs=(surface, surface, surface, blocked, blocked),
        out_specs=(surface, blocked),
        check_vma=False,
    )
```
